128 devices in a mesh: cand: 16 (over x, y), dom: 8 (over z, core).
Axes of the slice: x: 4, y: 4, z: 4, core: 2. Of those that a mesh axis runs over, the one named last changes fastest.
Arguments:
- strain_ops: bfloat16 [4, 6, 30, 131072], P(None, None, None, ('cand', 'dom')), may hold values from -0.109375 to 0.109375
- elem_scale: float32 [4, 131072], P(None, ('cand', 'dom')), may hold values from 0.5 to 2
- moduli: float32 [2, 131072], P(None, ('cand', 'dom')), may hold values from 0.5 to 2
- elem_block: int32 [131072, 1], P(('cand', 'dom')), may hold values from 0 to 127, as said below
- elem_slot: int32 [131072], P(('cand', 'dom')), may hold values from 0 to 11
- mass: float32 [8, 6144], P('dom', 'cand'), may hold values from 0.5 to 2
- updates: bfloat16 [8, 6144, 256], P('dom', 'cand'), may hold values from -6 to 6
Outputs:
- factor: float32 [8, 6144, 6144], P('dom', 'cand')
The draws below stay inside these ranges and needn't reach their ends.
Inputs may be any that keep to these rules, and one draw needn't show every extreme that they name: `elem_block`: the elements of the device at index c of cand and d of dom, with i = c * 8 + d, go to the blocks i - o modulo 128 for o in 0, 1, 2, 3, 8, 9, 64 and 65. Of the 1024 elements of one device, at most 256 go to one block, and every device sends exactly 256 to one of its blocks.
All inputs are finite; a program needn't handle non-finite values.
Results may differ from the reference program's by a relative error of at most 0.0003.
Values may be sent and summed in bfloat16 or wider, within the bound.
No kernel may reach another device: no remote copies, remote signals or barrier semaphores. Data moves between devices by JAX's collectives and lax.ppermute only.
A program may use at most 192 MiB of HBM per device.

```python
import math
import jax
import jax.numpy as jnp
import numpy as np
from jax import lax

W = 384
R = 256
QUAD = 4
KSTEPS = 2
E_DEV = 1024
SLOTS = 12
M = 6144
ELEMS = 131072
N_CAND = 16
N_DOM = 8
DEVICES = 128


def draw_elem_block(key, part):
    key = jax.random.fold_in(key, 11)
    quarter = E_DEV // 16
    shares = np.array([4, 2, 2, 2, 2, 2, 1, 1]) * quarter
    units = jnp.asarray(np.repeat(np.arange(8), shares).astype(np.int32))
    device = jnp.arange(DEVICES, dtype=jnp.int32)
    offsets = jnp.asarray(np.array([0, 1, 2, 3, N_DOM, N_DOM + 1, DEVICES // 2, DEVICES // 2 + 1]).astype(np.int32))
    targets = (device[:, None] - offsets[None, :] + DEVICES) % DEVICES
    keys = jax.random.split(key, DEVICES)

    def one_device(dev_key, dev_targets):
        first_key, second_key = jax.random.split(dev_key)
        order = jax.random.permutation(first_key, 8)
        placed = dev_targets[order][units]
        return placed[jax.random.permutation(second_key, E_DEV)]
    blocks = jax.vmap(one_device)(keys, targets)
    return blocks.reshape(DEVICES * E_DEV, 1).astype(jnp.int32)


def plant(drawn, stream_key, smallest, top_value):
    spot = [jax.random.randint(jax.random.fold_in(stream_key, axis), (), 0, length) for axis, length in enumerate(drawn.shape)]
    longest = drawn.shape.index(max(drawn.shape))
    beside = spot[:longest] + [(spot[longest] + 1) % drawn.shape[longest]] + spot[longest + 1:]
    return drawn.at[tuple(spot)].set(smallest).at[tuple(beside)].set(top_value)


def steps_of(own_key, extent, cuts, low, largest):
    loudness = 1.0
    for axis_at, blocks in cuts:
        steps = jax.random.uniform(jax.random.fold_in(jax.random.fold_in(own_key, 6), axis_at), (blocks,), jnp.float32, low / len(cuts), largest / len(cuts))
        loudness = loudness * jnp.repeat(jnp.exp(steps), extent[axis_at] // blocks).reshape((-1,) + (1,) * (len(extent) - 1 - axis_at))
    return loudness


def centred(stream_key, shape, deviation, limit, cuts=(), kind=jnp.bfloat16):
    level = steps_of(stream_key, shape, cuts, -0.22, 0.18) if cuts else 1.0
    entries = jax.random.normal(stream_key, shape, jnp.float32) * deviation * level
    return jnp.minimum(jnp.maximum(entries, -limit), limit).astype(kind)


def setup_inputs(seed: int = 0) -> dict:
    key_list = jax.random.split(jax.random.key(seed), 8)
    return {
        "strain_ops": centred(key_list[0], (QUAD, 6, 30, ELEMS), (36 * E_DEV // SLOTS) ** -0.5, 0.109375, ((3, 128),)),
        "elem_scale": jnp.clip(jnp.exp(math.log(2.0) - 1.3862944 * jax.random.uniform(key_list[1], (QUAD, ELEMS), jnp.float32) ** steps_of(key_list[1], (QUAD, ELEMS), ((1, 128),), -0.2, 0.2)), 0.5, 2.0),
        "moduli": jnp.clip(jnp.exp(math.log(2.0) - 1.3862944 * jax.random.uniform(key_list[2], (2, ELEMS), jnp.float32) ** steps_of(key_list[2], (2, ELEMS), ((1, 128),), -0.2, 0.2)), 0.5, 2.0),
        "elem_block": draw_elem_block(jax.random.fold_in(key_list[7], 71), 0),
        "elem_slot": plant(jax.random.randint(key_list[4], (ELEMS,), 0, SLOTS), jax.random.fold_in(key_list[4], 1), 0, SLOTS - 1).astype(jnp.int32),
        "mass": jnp.clip(jnp.exp(math.log(2.0) - 1.3862944 * jax.random.uniform(key_list[5], (N_DOM, M), jnp.float32) ** steps_of(key_list[5], (N_DOM, M), ((0, 8), (1, 16)), -0.2, 0.2)), 0.5, 2.0),
        "updates": centred(key_list[6], (N_DOM, M, R), 1.0, 6.0, ((0, 8), (1, 16))),
    }


HIGHEST_PREC = lax.Precision.HIGHEST

def element_blocks(strain, scale, moduli):
    as_float = strain.astype(jnp.float32)
    weighted = as_float * (scale * moduli[0][None, :])[:, None, None, :]
    stiffness = jnp.einsum('qsie,qsje->ije', weighted, as_float, precision=HIGHEST_PREC)
    diverge = as_float[:, 0] + as_float[:, 1] + as_float[:, 2]
    stiffness = stiffness + jnp.einsum('qie,qje->ije', diverge * (scale * moduli[1][None, :])[:, None, :], diverge, precision=HIGHEST_PREC)
    padded = jnp.pad(stiffness, ((0, 2), (0, 2), (0, 0)))
    return padded.reshape(1024, stiffness.shape[2])

def reference(strain_ops, elem_scale, moduli, elem_block, elem_slot, mass, updates):
    tile_count = DEVICES * SLOTS
    target = elem_block[:, 0] * SLOTS + elem_slot

    def accumulate(running, block_index):
        first_elem = block_index * E_DEV
        strain = lax.dynamic_slice_in_dim(strain_ops, first_elem, E_DEV, 3)
        scale = lax.dynamic_slice_in_dim(elem_scale, first_elem, E_DEV, 1)
        mods = lax.dynamic_slice_in_dim(moduli, first_elem, E_DEV, 1)
        stiff_flat = element_blocks(strain, scale, mods)
        where_to = lax.dynamic_slice_in_dim(target, first_elem, E_DEV, 0)
        picks = (where_to[:, None] == jnp.arange(tile_count, dtype=jnp.int32)[None, :]).astype(jnp.float32)
        term = lax.dot_general(picks, stiff_flat, (((0,), (1,)), ((), ())), precision=HIGHEST_PREC)
        return (running + term, None)
    tile_sums, unused = lax.scan(accumulate, jnp.zeros((tile_count, 1024), jnp.float32), jnp.arange(DEVICES, dtype=jnp.int32))
    tile_total = N_CAND * SLOTS
    tile_sums = tile_sums.reshape(N_CAND, N_DOM, SLOTS, 32, 32)
    tile_sums = jnp.transpose(tile_sums, (1, 0, 2, 3, 4)).reshape(N_DOM, tile_total, 32, 32)

    def factor_one(pieces):
        tiles_g, mass_g, upd_g = pieces
        coupling = jnp.dot(upd_g.astype(jnp.float32), upd_g.T.astype(jnp.float32), preferred_element_type=jnp.float32) / R
        identity = jnp.eye(tile_total, dtype=jnp.float32)
        blocks = (identity[:, None, :, None] * tiles_g[:, :, None, :]).reshape(M, M)
        matrix = coupling + blocks + jnp.diag(mass_g)
        lead_width = KSTEPS * W
        lead_factor = jnp.linalg.cholesky(matrix[:lead_width, :lead_width])
        lower = lax.linalg.triangular_solve(lead_factor, matrix[lead_width:, :lead_width], left_side=False, lower=True, transpose_a=True)
        complement = matrix[lead_width:, lead_width:] - jnp.dot(lower, lower.T, precision=HIGHEST_PREC)
        upper_rows = jnp.concatenate([lead_factor, jnp.zeros((lead_width, M - lead_width), jnp.float32)], axis=1)
        lower_rows = jnp.concatenate([lower, complement], axis=1)
        return jnp.concatenate([upper_rows, lower_rows], axis=0)
    return lax.map(factor_one, (tile_sums, mass, updates))
```

```python
import jax
import jax.numpy as jnp
from jax import lax
from jax.experimental import pallas as pl
from jax.experimental.pallas import tpu as pltpu
from jax.sharding import PartitionSpec as P

F32 = jnp.float32
BF16 = jnp.bfloat16
W = 384
WINDOW = 768
RANK = 256
SLOTS = 12
TILE = 1024
CHUNK = 256
SHIFTS = (0, 1, 3, 2)
BINS = {0: 0, 8: 12, 64: 24, 1: 40, 9: 52, 65: 64, 2: 80, 3: 96}
BIN_ROWS = 112


def split3(x):
    a = x.astype(BF16); r = x - a.astype(F32)
    b = r.astype(BF16); c = (r - b.astype(F32)).astype(BF16)
    return a, b, c


def dot_nn(a, b): return lax.dot_general(a, b, (((1,), (0,)), ((), ())), preferred_element_type=F32)
def dot_nt(a, b): return lax.dot_general(a, b, (((1,), (1,)), ((), ())), preferred_element_type=F32)


def product_tn(x, y):
    xt = x.T
    x1, x2, x3 = split3(xt)
    y1, y2, y3 = split3(y)
    left = jnp.concatenate([x1, x1, x2, x1, x2, x3], axis=1)
    right = jnp.concatenate([y1, y2, y1, y3, y2, y1], axis=0)
    return dot_nn(left, right)


def eliminate(rows, first):
    sub = lax.broadcasted_iota(jnp.int32, (8, 128), 0)
    n = len(rows)
    for t in range(n):
        c0 = first + 8 * t
        cols = {q: [jnp.broadcast_to(rows[q][0][:, c0 + k:c0 + k + 1], (8, 128)) for k in range(8)] for q in range(t, n)}
        for k in range(8):
            pivot = jnp.broadcast_to(cols[t][k][k:k + 1, :], (8, 128))
            rs = lax.rsqrt(pivot)
            f = {q: cols[q][k] * rs for q in range(t, n)}
            for m in range(k + 1, 8):
                sm = jnp.broadcast_to(f[t][m:m + 1, :], (8, 128))
                for q in range(t, n):
                    cols[q][m] = cols[q][m] - f[q] * sm
            fm = jnp.where(sub > k, f[t], 0.0)
            for h in range(len(rows[t])):
                r = jnp.broadcast_to(rows[t][h][k:k + 1, :], (8, 128)) * rs
                rows[t][h] = jnp.where(sub == k, r, rows[t][h] - fm * r)
                for q in range(t + 1, n):
                    rows[q][h] = rows[q][h] - f[q] * r
    return rows


def unpack_tiles(packed, out_ref):
    n = packed.shape[0]
    lane = lax.broadcasted_iota(jnp.int32, (n, 128), 1) // 32
    tile = lax.broadcasted_iota(jnp.int32, (n, 128), 0) % 4
    for g in range(8):
        x = packed[:, 128 * g:128 * g + 128]
        turned = [x] + [pltpu.roll(x, 32 * r, 1) for r in range(1, 4)]
        for u in range(4):
            row = jnp.zeros((n, 128), F32)
            for v in range(4):
                row = jnp.where((lane == v) & (tile == v), turned[(v - u) % 4], row)
            out_ref[pl.ds(4 * g + u, n, stride=32), :] = row


def stiffness_kernel(strain, scale, moduli, bins, mass, keep, far, two, three, plain, weighted, high, low, total):
    step = pl.program_id(0)

    @pl.when(step == 0)
    def _():
        plain[...] = jnp.zeros_like(plain)
        weighted[...] = jnp.zeros_like(weighted)
        high[...] = jnp.zeros_like(high)
        low[...] = jnp.zeros_like(low)
        total[...] = jnp.zeros_like(total)
        lane = lax.broadcasted_iota(jnp.int32, (SLOTS, TILE), 1)
        spread = jnp.concatenate([mass[...]] * 32, axis=1)
        total[:SLOTS, :] = jnp.where(lane // 32 == lane % 32, spread, 0.0)

    for part in range(CHUNK // 128):
        at = slice(128 * part, 128 * part + 128)
        for q in range(4):
            weight = scale[q:q + 1, at]
            shear = weight * moduli[0:1, at]
            bulk = weight * moduli[1:2, at]
            diverge = None
            for s in range(6):
                b = strain[q, s, :, at].astype(F32)
                plain[7 * q + s, :30, :] = b
                weighted[7 * q + s, :30, :] = b * shear
                if s < 3:
                    diverge = b if s == 0 else diverge + b
            plain[7 * q + 6, :30, :] = diverge
            weighted[7 * q + 6, :30, :] = diverge * bulk
        for a in range(4):
            rows = range(8 * a, min(8 * a + 8, 30))
            sums = {}
            for n in range(28):
                right = weighted[n, 8 * a:, :]
                for i in rows:
                    term = plain[n, i:i + 1, :] * right
                    sums[i] = term if n == 0 else sums[i] + term
            for i in rows:
                k = sums[i]
                if a:
                    k = jnp.concatenate([jnp.zeros((8 * a, 128), F32), k], axis=0)
                top = k.astype(BF16)
                high[32 * i:32 * i + 32, at] = top
                low[32 * i:32 * i + 32, at] = (k - top.astype(F32)).astype(BF16)
    chosen = lax.broadcasted_iota(jnp.int32, (BIN_ROWS, CHUNK), 0) == bins[...]
    chosen = chosen.astype(F32).astype(BF16)
    total[...] += dot_nt(chosen, high[...]) + dot_nt(chosen, low[...])

    @pl.when(step == pl.num_programs(0) - 1)
    def _():
        keep[...] = total[0:40, :]
        far[...] = total[40:80, :]
        two[...] = total[80:96, :]
        three[...] = total[96:112, :]


def stiffness_tiles(strain, scale, moduli, bins, mass):
    steps = strain.shape[3] // CHUNK
    whole = lambda rows: pl.BlockSpec((rows, TILE), lambda i: (0, 0))
    return pl.pallas_call(
        stiffness_kernel,
        grid=(steps,),
        in_specs=[
            pl.BlockSpec((4, 6, 30, CHUNK), lambda i: (0, 0, 0, i)),
            pl.BlockSpec((4, CHUNK), lambda i: (0, i)),
            pl.BlockSpec((2, CHUNK), lambda i: (0, i)),
            pl.BlockSpec((1, CHUNK), lambda i: (0, i)),
            pl.BlockSpec((SLOTS, 32), lambda i: (0, 0)),
        ],
        out_specs=[whole(40), whole(40), whole(16), whole(16)],
        out_shape=[jax.ShapeDtypeStruct((r, TILE), F32) for r in (40, 40, 16, 16)],
        scratch_shapes=[
            pltpu.VMEM((28, 32, 128), F32),
            pltpu.VMEM((28, 32, 128), F32),
            pltpu.VMEM((TILE, CHUNK), BF16),
            pltpu.VMEM((TILE, CHUNK), BF16),
            pltpu.VMEM((BIN_ROWS, TILE), F32),
        ],
        compiler_params=pltpu.CompilerParams(vmem_limit_bytes=32 * 2**20),
        name="stiffness_tiles",
    )(strain, scale, moduli, bins, mass)


def mirror(block):
    row = lax.broadcasted_iota(jnp.int32, block.shape, 0) // 8
    col = lax.broadcasted_iota(jnp.int32, block.shape, 1) // 8
    return jnp.where(row <= col, block, block.T)


def factor_window(diag, v_ref, h_ref, m_ref, work):
    square = lambda n, dim: lax.broadcasted_iota(jnp.int32, (n, n), dim)
    m_ref[...] = (square(256, 0) == square(256, 1)).astype(F32)
    upper = square(128, 0) <= square(128, 1)

    def block(j, carry):
        at = pl.ds(pl.multiple_of(j * 128, 128), 128)
        v = v_ref[at, :]
        m1, m2, m3 = split3(m_ref[...])
        p = dot_nn(v, m1) + (dot_nn(v, m2) + dot_nn(v, m3))
        p1, p2, p3 = split3(p)
        work[:, :128] = mirror(diag[at, :]) + (dot_nt(p1, v) + (dot_nt(p2, v) + dot_nt(p3, v)))
        work[:, 128:] = p
        for s in range(4):
            at_row = lambda q: slice(32 * s + 8 * q, 32 * s + 8 * q + 8)
            rows = [[work[at_row(q), 128 * h:128 * h + 128] for h in range(3)] for q in range(4)]
            rows = eliminate(rows, 32 * s)
            for q in range(4):
                for h in range(3):
                    work[at_row(q), 128 * h:128 * h + 128] = rows[q][h]
            if s < 3:
                done = work[32 * s:32 * s + 32, :]
                change = product_tn(done[:, :128], done)
                work[32 * s + 32:, :] = work[32 * s + 32:, :] - change[32 * s + 32:, :]
        h = work[:, 128:]
        h_ref[at, :] = h
        diag[at, :] = jnp.where(upper, work[:, :128], 0.0).T
        m_ref[...] = m_ref[...] - product_tn(h, h)
        return carry

    lax.fori_loop(0, WINDOW // 128, block, 0)


def kept_at(shift):
    return jnp.where(shift == 3, 2, jnp.where(shift == 2, 3, shift))


def factor_kernel(place, lead, own_tiles, own, *refs):
    left, right = refs[0:4], refs[4:8]
    out = refs[8]
    diag, own_diag, v_ref, h_ref, m_ref, work, panel, blocks, sems = refs[9:]
    x, y = place[0], place[1]
    cand = 4 * x + y

    unpack_tiles(lead[...], diag)
    unpack_tiles(own_tiles[...], own_diag)
    kept_x = kept_at(x)
    for b in range(2):
        shift_y = lax.rem(y - b + 4, 4)
        kept_y = kept_at(shift_y)
        for n, shift in enumerate(SHIFTS):
            @pl.when(shift_y == shift)
            def _():
                v_ref[W * b:W * b + W, :128] = left[n][kept_x] * 0.0625

            @pl.when(x == shift)
            def _():
                v_ref[W * b:W * b + W, 128:] = right[n][kept_y] * 0.0625
    factor_window(diag, v_ref, h_ref, m_ref, work)

    v_own = own[...] * 0.0625
    m1, m2, m3 = split3(m_ref[...])
    q = (dot_nn(v_own, m1) + (dot_nn(v_own, m2) + dot_nn(v_own, m3))) * 0.0625
    q1 = q.astype(BF16)
    q2 = (q - q1.astype(F32)).astype(BF16)
    h = h_ref[...]
    h1 = h.astype(BF16)
    h2 = (h - h1.astype(F32)).astype(BF16)
    panel[...] = dot_nt(v_own, h1) + dot_nt(v_own, h2)

    @pl.when(cand < 2)
    def _():
        row = lax.broadcasted_iota(jnp.int32, (W, WINDOW), 0) // 128 + 3 * cand
        col = lax.broadcasted_iota(jnp.int32, (W, WINDOW), 1) // 128
        panel[...] = jnp.where(row > col, panel[...], 0.0)
        for a in range(3):
            rows = pl.ds(pl.multiple_of(W * cand + 128 * a, 128), 128)
            panel[128 * a:128 * a + 128, rows] = diag[rows, :]

    lead_copy = pltpu.make_async_copy(panel, out.at[0, :, pl.ds(0, WINDOW)], sems.at[16])
    lead_copy.start()

    copies = []
    for n, shift_y in enumerate(SHIFTS):
        for m, shift_x in enumerate(SHIFTS):
            column = 4 * lax.rem(x - shift_x + 4, 4) + lax.rem(y - shift_y + 4, 4)
            slot = 4 * n + m
            copy = pltpu.make_async_copy(
                blocks.at[slot],
                out.at[0, :, pl.ds(pl.multiple_of(column * W, 128), W)],
                sems.at[slot],
            )
            copies.append((column, copy))

            @pl.when(column >= 2)
            def _():
                @pl.when(cand < 2)
                def _():
                    blocks[slot] = jnp.zeros((W, W), F32)

                @pl.when(cand >= 2)
                def _():
                    v = jnp.concatenate([left[n][m], right[m][n]], axis=1)
                    blocks[slot] = dot_nt(q1, v) + dot_nt(q2, v)
                    if slot == 0:
                        for a in range(3):
                            at = slice(128 * a, 128 * a + 128)
                            blocks[slot, at, at] += mirror(own_diag[at, :])

                copy.start()
    lead_copy.wait()
    for column, copy in copies:
        @pl.when(column >= 2)
        def _():
            copy.wait()


def factor_rows(place, lead, own_tiles, own, left, right):
    vmem = pl.BlockSpec(memory_space=pltpu.VMEM)
    return pl.pallas_call(
        factor_kernel,
        in_specs=[pl.BlockSpec(memory_space=pltpu.SMEM)] + [vmem] * 11,
        out_specs=pl.BlockSpec(memory_space=pl.ANY),
        out_shape=jax.ShapeDtypeStruct((1, W, 16 * W), F32),
        scratch_shapes=[
            pltpu.VMEM((WINDOW, 128), F32),
            pltpu.VMEM((W, 128), F32),
            pltpu.VMEM((WINDOW, RANK), BF16),
            pltpu.VMEM((WINDOW, RANK), F32),
            pltpu.VMEM((RANK, RANK), F32),
            pltpu.VMEM((128, 128 + RANK), F32),
            pltpu.VMEM((W, WINDOW), F32),
            pltpu.VMEM((16, W, W), F32),
            pltpu.SemaphoreType.DMA((17,)),
        ],
        compiler_params=pltpu.CompilerParams(vmem_limit_bytes=40 * 2**20),
        name="factor_rows",
    )(place, lead, own_tiles, own, *left, *right)


def move_x(value, shift):
    return lax.ppermute(value, "cand", [(4 * x + y, (x + shift) % 4 * 4 + y) for x in range(4) for y in range(4)])


def move_y(value, shift):
    return lax.ppermute(value, "cand", [(4 * x + y, 4 * x + (y + shift) % 4) for x in range(4) for y in range(4)])


def move_back(value, offset):
    return lax.ppermute(value, ("cand", "dom"), [(i, (i - offset) % 128) for i in range(128)])


def local(strain_ops, elem_scale, moduli, elem_block, elem_slot, mass, updates):
    cand = lax.axis_index("cand")
    device = cand * lax.axis_size("dom") + lax.axis_index("dom")
    own = updates[0]

    left = jnp.stack([own[:, :128]] + [move_x(own[:, :128], s) for s in SHIFTS[1:]])
    right = jnp.stack([own[:, 128:]] + [move_y(own[:, 128:], s) for s in SHIFTS[1:]])
    left = [left] + [move_y(left, s) for s in SHIFTS[1:]]
    right = [right] + [move_x(right, s) for s in SHIFTS[1:]]

    offset = (device - elem_block[:, 0]) & 127
    first = jnp.zeros_like(offset)
    for o, start in BINS.items():
        first = jnp.where(offset == o, start, first)
    bins = (first + elem_slot)[None, :]
    keep, far, two, three = stiffness_tiles(strain_ops, elem_scale, moduli, bins, mass.reshape(SLOTS, 32))

    far = move_back(far, 1)
    two = move_back(two, 2)
    three = move_back(three, 3)
    here = keep[:12] + far[:12] + two[:12] + three[:12]
    near = keep[12:24] + far[12:24]
    half = keep[24:36] + far[24:36]
    zero = jnp.zeros_like(here)
    pick = lambda c: jnp.where(cand == c, here, jnp.where(cand == c + 1, near, jnp.where(cand == c + 8, half, zero)))
    lead = jnp.concatenate([pick(0), pick(1)], axis=0)
    for bit in (1, 2, 4, 8):
        lead = lead + lax.ppermute(lead, "cand", [(i, i ^ bit) for i in range(16)])
    own_tiles = here + move_back(near, 8) + move_back(half, 64)
    place = jnp.stack([cand // 4, cand % 4]).astype(jnp.int32)
    return factor_rows(place, lead, own_tiles, own, left, right)


def solution(mesh):
    placed = (
        P(None, None, None, ("cand", "dom")),
        P(None, ("cand", "dom")),
        P(None, ("cand", "dom")),
        P(("cand", "dom"), None),
        P(("cand", "dom")),
        P("dom", "cand"),
        P("dom", "cand", None),
    )
    return jax.shard_map(
        local, mesh=mesh, in_specs=placed, out_specs=P("dom", "cand", None), check_vma=False
    )
```

```python
import functools

import jax
import jax.numpy as jnp
from jax import lax
from jax.experimental import pallas as pl
from jax.experimental.pallas import tpu as pltpu
from jax.sharding import PartitionSpec as P

F32 = jnp.float32
BF16 = jnp.bfloat16
W = 384
WINDOW = 768
PARTS = ((0, 512), (512, 256))
RANK = 256
SLOTS = 12
TILE = 1024
CHUNK = 256
ACROSS = (0, 1, 3, 2)
BINS = {0: 0, 8: 12, 64: 24, 1: 40, 9: 52, 65: 64, 2: 80, 3: 96}
BIN_ROWS = 112


def split3(x):
    a = x.astype(BF16); r = x - a.astype(F32)
    b = r.astype(BF16); c = (r - b.astype(F32)).astype(BF16)
    return a, b, c


def dot_nn(a, b): return lax.dot_general(a, b, (((1,), (0,)), ((), ())), preferred_element_type=F32)
def dot_nt(a, b): return lax.dot_general(a, b, (((1,), (1,)), ((), ())), preferred_element_type=F32)


def product_tn(x, y):
    x1, x2, x3 = split3(x)
    y1, y2, y3 = split3(y)
    left = jnp.concatenate([x1, x1, x2, x1, x2, x3], axis=0)
    right = jnp.concatenate([y1, y2, y1, y3, y2, y1], axis=0)
    return lax.dot_general(left, right, (((0,), (0,)), ((), ())), preferred_element_type=F32)


def eliminate(rows, first):
    sub = lax.broadcasted_iota(jnp.int32, (8, 128), 0)
    n = len(rows)
    spread = lambda x, at: jnp.broadcast_to(x[at:at + 1, :], (8, 128))
    cols = {}
    for k in range(8 * n):
        for q in range(k // 8, n):
            cols[q, k] = jnp.broadcast_to(rows[q][0][:, first + k:first + k + 1], (8, 128))
    for k in range(8 * n):
        t, u = k // 8, k % 8
        rs = lax.rsqrt(spread(cols[t, k], u))
        f = {q: cols[q, k] * rs for q in range(t, n)}
        for m in range(k + 1, 8 * n):
            sm = spread(f[m // 8], m % 8)
            for q in range(m // 8, n):
                cols[q, m] = cols[q, m] - f[q] * sm
        fm = jnp.where(sub > u, f[t], 0.0)
        for h in range(len(rows[t])):
            r = spread(rows[t][h], u) * rs
            rows[t][h] = jnp.where(sub == u, r, rows[t][h] - fm * r)
            for q in range(t + 1, n):
                rows[q][h] = rows[q][h] - f[q] * r
    return rows


def unpack_tiles(packed, out_ref):
    n = packed.shape[0]
    lane = lax.broadcasted_iota(jnp.int32, (n, 128), 1) // 32
    tile = lax.broadcasted_iota(jnp.int32, (n, 128), 0) % 4
    for g in range(8):
        x = packed[:, 128 * g:128 * g + 128]
        turned = [x] + [pltpu.roll(x, 32 * r, 1) for r in range(1, 4)]
        for u in range(4):
            row = jnp.zeros((n, 128), F32)
            for v in range(4):
                row = jnp.where((lane == v) & (tile == v), turned[(v - u) % 4], row)
            out_ref[pl.ds(4 * g + u, n, stride=32), :] = row


def stiffness_kernel(first, strain, scale, moduli, bins, begin, *refs):
    outs, (plain, weighted, high, low, total, data, sems) = refs[:-7], refs[-7:]
    steps = data.shape[0]
    copies = []
    for n in range(steps):
        at = pl.ds((first + n) * CHUNK, CHUNK)
        copies.append(pltpu.make_async_copy(strain.at[:, :, :, at], data.at[n], sems.at[n]))
        copies[n].start()
    plain[...] = jnp.zeros_like(plain)
    weighted[...] = jnp.zeros_like(weighted)
    high[...] = jnp.zeros_like(high)
    low[...] = jnp.zeros_like(low)
    if first:
        total[...] = begin[...]
    else:
        total[...] = jnp.zeros_like(total)
        lane = lax.broadcasted_iota(jnp.int32, (SLOTS, TILE), 1)
        spread = jnp.concatenate([begin[...]] * 32, axis=1)
        total[:SLOTS, :] = jnp.where(lane // 32 == lane % 32, spread, 0.0)

    for step in range(steps):
        copies[step].wait()

        def one_part(part, carry):
            here = pl.multiple_of(128 * part, 128)
            at = pl.ds(here, 128)
            there = pl.ds(pl.multiple_of((first + step) * CHUNK + here, 128), 128)
            for q in range(4):
                weight = scale[q:q + 1, there]
                shear = weight * moduli[0:1, there]
                bulk = weight * moduli[1:2, there]
                diverge = None
                for s in range(6):
                    b = data[step, q, s, :, at].astype(F32)
                    plain[7 * q + s, :30, :] = b
                    weighted[7 * q + s, :30, :] = b * shear
                    if s < 3:
                        diverge = b if s == 0 else diverge + b
                plain[7 * q + 6, :30, :] = diverge
                weighted[7 * q + 6, :30, :] = diverge * bulk
            for a in range(4):
                rows = range(8 * a, min(8 * a + 8, 30))
                sums = {}
                for n in range(28):
                    right = weighted[n, 8 * a:, :]
                    for i in rows:
                        term = plain[n, i:i + 1, :] * right
                        sums[i] = term if n == 0 else sums[i] + term
                for i in rows:
                    k = sums[i]
                    if a:
                        k = jnp.concatenate([jnp.zeros((8 * a, 128), F32), k], axis=0)
                    top = k.astype(BF16)
                    high[32 * i:32 * i + 32, at] = top
                    low[32 * i:32 * i + 32, at] = (k - top.astype(F32)).astype(BF16)
            return carry

        lax.fori_loop(0, CHUNK // 128, one_part, 0)
        chosen = lax.broadcasted_iota(jnp.int32, (BIN_ROWS, CHUNK), 0) == bins[:, (first + step) * CHUNK:(first + step + 1) * CHUNK]
        chosen = chosen.astype(F32).astype(BF16)
        total[...] += dot_nt(chosen, high[...]) + dot_nt(chosen, low[...])

    at = 0
    for out in outs:
        out[...] = total[at:at + out.shape[0], :]
        at += out.shape[0]


def stiffness_tiles(first, steps, strain, scale, moduli, bins, begin, outs):
    vmem = pl.BlockSpec(memory_space=pltpu.VMEM)
    return pl.pallas_call(
        functools.partial(stiffness_kernel, first),
        in_specs=[pl.BlockSpec(memory_space=pltpu.HBM)] + [vmem] * 4,
        out_specs=[vmem] * len(outs),
        out_shape=[jax.ShapeDtypeStruct((r, TILE), F32) for r in outs],
        scratch_shapes=[
            pltpu.VMEM((28, 32, 128), F32),
            pltpu.VMEM((28, 32, 128), F32),
            pltpu.VMEM((TILE, CHUNK), BF16),
            pltpu.VMEM((TILE, CHUNK), BF16),
            pltpu.VMEM((BIN_ROWS, TILE), F32),
            pltpu.VMEM((steps, 4, 6, 30, CHUNK), BF16),
            pltpu.SemaphoreType.DMA((steps,)),
        ],
        cost_estimate=pl.CostEstimate(flops=5 * 10**9, bytes_accessed=15 * 10**6, transcendentals=0),
        compiler_params=pltpu.CompilerParams(vmem_limit_bytes=32 * 2**20),
        name="stiffness_tiles",
    )(strain, scale, moduli, bins, begin)


def mirror(block):
    row = lax.broadcasted_iota(jnp.int32, block.shape, 0) // 8
    col = lax.broadcasted_iota(jnp.int32, block.shape, 1) // 8
    return jnp.where(row <= col, block, block.T)


def factor_window(diag, v_ref, h_ref, m_ref, work):
    square = lambda n, dim: lax.broadcasted_iota(jnp.int32, (n, n), dim)
    upper = square(128, 0) <= square(128, 1)

    def block(j, carry):
        at = pl.ds(pl.multiple_of(j * 128, 128), 128)
        v = v_ref[at, :]
        m1, m2, m3 = split3(m_ref[...])
        p = dot_nn(v, m1) + (dot_nn(v, m2) + dot_nn(v, m3))
        p1, p2, p3 = split3(p)
        work[:, :128] = mirror(diag[at, :]) + (dot_nt(p1, v) + (dot_nt(p2, v) + dot_nt(p3, v)))
        work[:, 128:] = p
        for s in range(4):
            at_row = lambda q: slice(32 * s + 8 * q, 32 * s + 8 * q + 8)
            rows = [[work[at_row(q), 128 * h:128 * h + 128] for h in range(3)] for q in range(4)]
            rows = eliminate(rows, 32 * s)
            for q in range(4):
                for h in range(3):
                    work[at_row(q), 128 * h:128 * h + 128] = rows[q][h]
            if s < 3:
                done = work[32 * s:32 * s + 32, :]
                change = product_tn(done[:, :128], done)
                work[32 * s + 32:, :] = work[32 * s + 32:, :] - change[32 * s + 32:, :]
        h = work[:, 128:]
        h_ref[at, :] = h
        diag[at, :] = jnp.where(upper, work[:, :128], 0.0).T
        m_ref[...] = m_ref[...] - product_tn(h, h)
        return carry

    lax.fori_loop(0, diag.shape[0] // 128, block, 0)


def window_kernel(part, place, lead, v0, v1, v2, *refs):
    high_ref, low_ref, m_ref, diag, v_ref, h_ref, work = refs[-7:]
    first, size = PARTS[part]
    x = place[0] // 4
    for n, v in enumerate((v0, v1, v2)):
        @pl.when((x == n) | ((x == 3) & (n == 2)))
        def _():
            v_ref[...] = v[first:first + size, :] * 0.0625

    if part:
        m_ref[...] = refs[0][...]
    else:
        square = lambda dim: lax.broadcasted_iota(jnp.int32, (RANK, RANK), dim)
        m_ref[...] = (square(0) == square(1)).astype(F32)
    unpack_tiles(lead[first // 32:(first + size) // 32, :], diag)
    factor_window(diag, v_ref, h_ref, m_ref, work)
    h = h_ref[...]
    high = h.astype(BF16)
    high_ref[...] = high
    low_ref[...] = (h - high.astype(F32)).astype(BF16)


def window_factor(part, place, lead, v, m):
    vmem = pl.BlockSpec(memory_space=pltpu.VMEM)
    size = PARTS[part][1]
    return pl.pallas_call(
        functools.partial(window_kernel, part),
        in_specs=[pl.BlockSpec(memory_space=pltpu.SMEM)] + [vmem] * (4 + len(m)),
        out_specs=[vmem] * 4,
        out_shape=[
            jax.ShapeDtypeStruct((size, RANK), BF16),
            jax.ShapeDtypeStruct((size, RANK), BF16),
            jax.ShapeDtypeStruct((RANK, RANK), F32),
            jax.ShapeDtypeStruct((size, 128), F32),
        ],
        scratch_shapes=[
            pltpu.VMEM((size, RANK), BF16),
            pltpu.VMEM((size, RANK), F32),
            pltpu.VMEM((128, 128 + RANK), F32),
        ],
        cost_estimate=pl.CostEstimate(flops=size * 10**7, bytes_accessed=size * 10**5, transcendentals=0),
        compiler_params=pltpu.CompilerParams(vmem_limit_bytes=32 * 2**20),
        name="window_factor",
    )(place, lead, *v, *m)


def rows_kernel(place, high0, low0, diag0, high1, low1, m_ref, diag1, own_tiles, own, here, before, after, low, high, out, *scratch):
    own_diag, panel, blocks, sems = scratch
    cand = place[0]
    x, y = cand // 4, lax.rem(cand, 4)
    v_own = own[...] * 0.0625
    split = PARTS[1][0]
    panel[:, :split] = dot_nt(v_own, high0[...]) + dot_nt(v_own, low0[...])
    panel[:, split:] = dot_nt(v_own, high1[...]) + dot_nt(v_own, low1[...])
    for n in range(2):
        @pl.when(cand == n)
        def _():
            row = lax.broadcasted_iota(jnp.int32, (W, WINDOW), 0) // 128 + 3 * n
            col = lax.broadcasted_iota(jnp.int32, (W, WINDOW), 1) // 128
            panel[...] = jnp.where(row > col, panel[...], 0.0)
            for a in range(3):
                at = W * n + 128 * a
                diag = diag0[at:at + 128, :] if at < split else diag1[at - split:at - split + 128, :]
                panel[128 * a:128 * a + 128, at:at + 128] = diag

    panel_copy = pltpu.make_async_copy(panel, out.at[0, :, pl.ds(0, WINDOW)], sems.at[16])
    panel_copy.start()
    unpack_tiles(own_tiles[...], own_diag)
    m1, m2, m3 = split3(m_ref[...])
    q = (dot_nn(v_own, m1) + (dot_nn(v_own, m2) + dot_nn(v_own, m3))) * 0.0625
    q = jnp.where(cand < 2, 0.0, q)
    q1 = q.astype(BF16)
    q2 = (q - q1.astype(F32)).astype(BF16)
    stores = []
    for n, pieces in enumerate((here, before, after, (low, high))):
        column_x = lax.rem(x + (0, 3, 1, 2)[n], 4)
        for pair in range(2):
            v = pieces[pair][...] if n == 3 else pieces[2 * pair:2 * pair + 2]
            v = v.reshape(2 * W, RANK)
            slot = 2 * n + pair
            blocks[slot] = dot_nt(q1, v) + dot_nt(q2, v)
            if slot == 0:
                @pl.when(cand >= 2)
                def _():
                    for a in range(3):
                        at = slice(128 * a, 128 * a + 128)
                        blocks[0, at, at] += mirror(own_diag[at, :])

            for m in range(2):
                column = 4 * column_x + (y ^ ACROSS[2 * pair + m])
                copy = pltpu.make_async_copy(
                    blocks.at[slot, :, pl.ds(W * m, W)],
                    out.at[0, :, pl.ds(pl.multiple_of(column * W, 128), W)],
                    sems.at[2 * slot + m],
                )
                stores.append((column, copy))

                @pl.when(column >= 2)
                def _():
                    copy.start()
    panel_copy.wait()
    for column, copy in stores:
        @pl.when(column >= 2)
        def _():
            copy.wait()


def factor_rows(place, *operands):
    vmem = pl.BlockSpec(memory_space=pltpu.VMEM)
    return pl.pallas_call(
        rows_kernel,
        in_specs=[pl.BlockSpec(memory_space=pltpu.SMEM)] + [vmem] * len(operands),
        out_specs=pl.BlockSpec(memory_space=pltpu.HBM),
        out_shape=jax.ShapeDtypeStruct((1, W, 16 * W), F32),
        scratch_shapes=[
            pltpu.VMEM((W, 128), F32),
            pltpu.VMEM((W, WINDOW), F32),
            pltpu.VMEM((8, W, 2 * W), F32),
            pltpu.SemaphoreType.DMA((17,)),
        ],
        compiler_params=pltpu.CompilerParams(vmem_limit_bytes=40 * 2**20),
        name="factor_rows",
    )(place, *operands)


def move_x(value, shift, sources=range(4)):
    pairs = [(4 * x + y, 4 * ((x + shift) % 4) + y) for x in sources for y in range(4)]
    return lax.ppermute(value, "cand", pairs)


def swap(value, bits):
    return lax.ppermute(value, "cand", [(i, i ^ bits) for i in range(16)])


def move_back(value, offset):
    return lax.ppermute(value, ("cand", "dom"), [(i, (i - offset) % 128) for i in range(128)])


def local(strain_ops, elem_scale, moduli, elem_block, elem_slot, mass, updates):
    cand = lax.axis_index("cand")
    device = cand * lax.axis_size("dom") + lax.axis_index("dom")
    x, y = cand // 4, cand % 4
    own = updates[0]
    place = cand.astype(jnp.int32)[None]

    offset = (device - elem_block[:, 0]) & 127
    start = jnp.zeros_like(offset)
    for o, at in BINS.items():
        start = jnp.where(offset == o, at, start)
    bins = (start + elem_slot)[None, :]

    here = jnp.stack([own, swap(own, 1)])
    here, bins = lax.optimization_barrier((here, bins))
    here_far = swap(here, 3)
    tiles = stiffness_tiles(0, 4, strain_ops, elem_scale, moduli, bins, mass.reshape(SLOTS, 32), (40, 40, 16, 16))
    here = jnp.concatenate([here, here_far])
    (keep, far, two, three), here = lax.optimization_barrier((tiles, here))

    piece = lambda r: functools.reduce(lambda u, n: jnp.where(r == ACROSS[n], here[n], u), range(1, 4), here[0])
    window = jnp.concatenate([piece(y), piece(y ^ 1)])
    window_1 = move_x(window, 1, (0,))

    far = move_back(far, 1)
    two = move_back(two, 2)
    three = move_back(three, 3)
    kept = keep[:12] + far[:12] + two[:12] + three[:12]
    near = keep[12:24] + far[12:24]
    half = keep[24:36] + far[24:36]
    zero = jnp.zeros_like(kept)
    pick = lambda c: jnp.where(cand == c, kept, jnp.where(cand == c + 1, near, jnp.where(cand == c + 8, half, zero)))
    lead = jnp.concatenate([pick(0), pick(1)], axis=0)
    lead = lead + swap(lead, 1)
    lead, window_1 = lax.optimization_barrier((lead, window_1))
    window_2 = jnp.where(x == 0, window, window_1)
    window_2 = lax.ppermute(window_2, "cand", [(y, 12 + y) for y in range(4)] + [(4 + y, 8 + y) for y in range(4)])
    lead = lead + swap(lead, 3)
    lead = lead + swap(lead, 4)
    lead = lead + swap(lead, 12)
    lead, window_2, here, near, half = lax.optimization_barrier((lead, window_2, here, near, half))

    before, after = move_x(here, 1), move_x(here, 3)
    own_tiles = kept + move_back(near, 8) + move_back(half, 64)
    high0, low0, m, diag0 = window_factor(0, place, lead, (window, window_1, window_2), ())
    m, before, after = lax.optimization_barrier((m, before, after))
    low, high = move_x(before[:2], 1), move_x(after[2:], 3)
    high1, low1, m, diag1 = window_factor(1, place, lead, (window, window_1, window_2), (m,))
    return factor_rows(place, high0, low0, diag0, high1, low1, m, diag1, own_tiles, own, here, before, after, low, high)


def solution(mesh):
    placed = (
        P(None, None, None, ("cand", "dom")),
        P(None, ("cand", "dom")),
        P(None, ("cand", "dom")),
        P(("cand", "dom"), None),
        P(("cand", "dom")),
        P("dom", "cand"),
        P("dom", "cand", None),
    )
    return jax.shard_map(
        local, mesh=mesh, in_specs=placed, out_specs=P("dom", "cand", None), check_vma=False
    )
```

```python
import functools

import jax
import jax.numpy as jnp
from jax import lax
from jax.experimental import pallas as pl
from jax.experimental.pallas import tpu as pltpu
from jax.sharding import PartitionSpec as P

F32 = jnp.float32
BF16 = jnp.bfloat16
W = 384
WINDOW = 768
PARTS = ((0, 512), (512, 256))
RANK = 256
SLOTS = 12
TILE = 512
CHUNK = 256
ACROSS = (0, 1, 3, 2)
BINS = {0: 0, 8: 12, 64: 24, 1: 40, 9: 52, 65: 64, 2: 80, 3: 96}
BIN_ROWS = 112


def split3(x):
    a = x.astype(BF16); r = x - a.astype(F32)
    b = r.astype(BF16); c = (r - b.astype(F32)).astype(BF16)
    return a, b, c


def dot_nn(a, b): return lax.dot_general(a, b, (((1,), (0,)), ((), ())), preferred_element_type=F32)
def dot_nt(a, b): return lax.dot_general(a, b, (((1,), (1,)), ((), ())), preferred_element_type=F32)


def product_tn(x, y):
    x1, x2, x3 = split3(x)
    y1, y2, y3 = split3(y)
    left = jnp.concatenate([x1, x1, x2, x1, x2, x3], axis=0)
    right = jnp.concatenate([y1, y2, y1, y3, y2, y1], axis=0)
    return lax.dot_general(left, right, (((0,), (0,)), ((), ())), preferred_element_type=F32)


def eliminate(rows, first):
    sub = lax.broadcasted_iota(jnp.int32, (8, 128), 0)
    n = len(rows)
    spread = lambda x, at: jnp.broadcast_to(x[at:at + 1, :], (8, 128))
    cols = {}
    for k in range(8 * n):
        for q in range(k // 8, n):
            cols[q, k] = jnp.broadcast_to(rows[q][0][:, first + k:first + k + 1], (8, 128))
    for k in range(8 * n):
        t, u = k // 8, k % 8
        rs = lax.rsqrt(spread(cols[t, k], u))
        f = {q: cols[q, k] * rs for q in range(t, n)}
        for m in range(k + 1, 8 * n):
            sm = spread(f[m // 8], m % 8)
            for q in range(m // 8, n):
                cols[q, m] = cols[q, m] - f[q] * sm
        fm = jnp.where(sub > u, f[t], 0.0)
        for h in range(len(rows[t])):
            r = spread(rows[t][h], u) * rs
            rows[t][h] = jnp.where(sub == u, r, rows[t][h] - fm * r)
            for q in range(t + 1, n):
                rows[q][h] = rows[q][h] - f[q] * r
    return rows


def unpack_tiles(packed, out_ref):
    n = packed.shape[0]
    lane = lax.broadcasted_iota(jnp.int32, (n, 128), 1)
    tile = lax.broadcasted_iota(jnp.int32, (n, 128), 0) % 4
    here = lane // 32 == tile
    entry = lane % 32
    for g in range(4):
        x = packed[:, 128 * g:128 * g + 128]
        turned = [x] + [pltpu.roll(x, 32 * r, 1) for r in range(1, 4)]
        for u in range(4):
            slot = turned[(0 - u) % 4]
            for v in range(1, 4):
                slot = jnp.where(tile == v, turned[(v - u) % 4], slot)
            p = 4 * g + u
            rows = ((30, 30), (31, 30)) if p == 15 else ((p, p), (29 - p, -1))
            for i, shift in rows:
                keep = here & (entry >= i) & (entry < (30 if i < 30 else i + 1))
                moved = pltpu.roll(slot, shift % 128, 1) if shift % 128 else slot
                out_ref[pl.ds(i, n, stride=32), :] = jnp.where(keep, moved, 0.0)


def stiffness_kernel(begin, strain, small, code, *refs):
    outs = refs[:-7] if begin == 0 else refs[1:-7]
    plain, weighted, sums, total, bins, data, sems = refs[-7:]
    steps = data.shape[0]
    copies = [
        pltpu.make_async_copy(strain.at[:, :, :, pl.ds((begin + n) * CHUNK, CHUNK)], data.at[n], sems.at[n])
        for n in range(steps)
    ]
    for copy in copies:
        copy.start()
    sums[...] = jnp.zeros_like(sums)
    if begin:
        total[...] = refs[0][...]
    else:
        total[...] = jnp.zeros_like(total)
        entry = lax.broadcasted_iota(jnp.int32, (W, TILE), 1)
        slot, at = entry // 32, entry % 32
        diagonal = jnp.where(slot == 15, 30 + at, jnp.where(at == 0, slot, jnp.where(at == 30 - slot, 29 - slot, -1)))
        spread = (diagonal == lax.broadcasted_iota(jnp.int32, (W, TILE), 0) % 32).astype(F32).astype(BF16)
        own = lax.broadcasted_iota(jnp.int32, (16, W), 1) // 32 == lax.broadcasted_iota(jnp.int32, (16, W), 0)
        mass = small[6:7, :W]
        total[:16, :] = sum(dot_nn(part, spread) for part in split3(jnp.where(own, mass, 0.0)))
    device = lax.axis_index("cand") * lax.axis_size("dom") + lax.axis_index("dom")
    offset = (device - code[...] // 16) & 127
    start = jnp.zeros_like(offset)
    for o, first in BINS.items():
        start = jnp.where(offset == o, first, start)
    bins[...] = start + code[...] % 16
    sub = lax.broadcasted_iota(jnp.int32, (8, 128), 0)

    def both(x):
        return jnp.concatenate([x[:, :128], x[:, 128:]], axis=0)

    def fold(a, b, bit):
        even = (sub & bit) == 0
        return jnp.where(even, a, pltpu.roll(b, bit, 0)) + jnp.where(even, pltpu.roll(a, 8 - bit, 0), b)

    def one_step(step, carry):
        for n, copy in enumerate(copies):
            @pl.when(step == n)
            def _():
                copy.wait()

        lanes = pl.ds(pl.multiple_of((begin + step) * CHUNK, CHUNK), CHUNK)
        weight = small[0:4, lanes]
        shear = both(weight * small[4:5, lanes])
        bulk = both(weight * small[5:6, lanes])
        for s in range(6):
            b = data[step, s].astype(F32)
            plain[s, :, 0:4, :] = b[:, :, :128]
            plain[s, :, 4:8, :] = b[:, :, 128:]
        for i in range(30):
            b = [plain[s, i] for s in range(6)]
            diverge = b[0] + b[1] + b[2]
            plain[6, i] = diverge
            weighted[6, i] = diverge * bulk
            for s in range(6):
                weighted[s, i] = b[s] * shear

        for first in range(0, 15, 2):
            slots = [p for p in (first, first + 1) if p < 15]
            owners = sorted({i for p in slots for i in (p, 29 - p)})
            rows = {i: [plain[s, i] for s in range(7)] for i in owners}
            ready = {(p, 31): None for p in slots}
            for col in range(first, 30):
                right = [weighted[s, col] for s in range(7)]
                for p in slots:
                    for i, l in ((p, col - p), (29 - p, col + 1)):
                        if col < i:
                            continue
                        products = [rows[i][s] * right[s] for s in range(7)]
                        value = products[0]
                        for product in products[1:]:
                            value = value + product
                        ready[p, l] = value
                        group = [(p, 8 * (l // 8) + m) for m in range(8)]
                        if not all(key in ready for key in group):
                            continue
                        eight = [ready.pop(key) for key in group]
                        eight = [jnp.zeros((8, 128), F32) if e is None else e for e in eight]
                        fours = []
                        for h in range(2):
                            a, b, c, d = eight[4 * h:4 * h + 4]
                            fours.append(fold(fold(a, b, 1), fold(c, d, 1), 2))
                        low, high = fours
                        r = 32 * p + 8 * (l // 8)
                        sums[r:r + 8, :128] = jnp.where(sub < 4, low, pltpu.roll(high, 4, 0))
                        sums[r:r + 8, 128:] = jnp.where(sub < 4, pltpu.roll(low, 4, 0), high)
        values = sums[...]
        high = values.astype(BF16)
        low = (values - high.astype(F32)).astype(BF16)
        chosen = lax.broadcasted_iota(jnp.int32, (BIN_ROWS, CHUNK), 0) == bins[:, lanes]
        chosen = chosen.astype(F32).astype(BF16)
        total[...] += dot_nt(chosen, high) + dot_nt(chosen, low)
        return carry

    lax.fori_loop(0, steps, one_step, 0)
    at = 0
    for out in outs:
        out[...] = total[at:at + out.shape[0], :]
        at += out.shape[0]


def stiffness_tiles(begin, steps, strain, small, code, total, outs):
    vmem = pl.BlockSpec(memory_space=pltpu.VMEM)
    return pl.pallas_call(
        functools.partial(stiffness_kernel, begin),
        in_specs=[pl.BlockSpec(memory_space=pltpu.HBM)] + [vmem] * (2 + len(total)),
        out_specs=[vmem] * len(outs),
        out_shape=[jax.ShapeDtypeStruct((r, TILE), F32) for r in outs],
        scratch_shapes=[
            pltpu.VMEM((7, 30, 8, 128), F32),
            pltpu.VMEM((7, 30, 8, 128), F32),
            pltpu.VMEM((TILE, CHUNK), F32),
            pltpu.VMEM((BIN_ROWS, TILE), F32),
            pltpu.VMEM(code.shape, jnp.int32),
            pltpu.VMEM((steps, 6, 30, 4, CHUNK), BF16),
            pltpu.SemaphoreType.DMA((steps,)),
        ],
        cost_estimate=pl.CostEstimate(flops=5 * 10**9, bytes_accessed=15 * 10**6, transcendentals=0),
        compiler_params=pltpu.CompilerParams(vmem_limit_bytes=32 * 2**20),
        name="stiffness_tiles",
    )(strain, small, code, *total)


def mirror(block):
    row = lax.broadcasted_iota(jnp.int32, block.shape, 0)
    col = lax.broadcasted_iota(jnp.int32, block.shape, 1)
    return jnp.where(row <= col, block, block.T)


def factor_window(diag, v_ref, h_ref, m_ref, work):
    square = lambda n, dim: lax.broadcasted_iota(jnp.int32, (n, n), dim)
    upper = square(128, 0) <= square(128, 1)

    def block(j, carry):
        at = pl.ds(pl.multiple_of(j * 128, 128), 128)
        v = v_ref[at, :]
        m1, m2, m3 = split3(m_ref[...])
        p = dot_nn(v, m1) + (dot_nn(v, m2) + dot_nn(v, m3))
        p1, p2, p3 = split3(p)
        work[:, :128] = mirror(diag[at, :]) + (dot_nt(p1, v) + (dot_nt(p2, v) + dot_nt(p3, v)))
        work[:, 128:] = p
        for s in range(4):
            at_row = lambda q: slice(32 * s + 8 * q, 32 * s + 8 * q + 8)
            rows = [[work[at_row(q), 128 * h:128 * h + 128] for h in range(3)] for q in range(4)]
            rows = eliminate(rows, 32 * s)
            for q in range(4):
                for h in range(3):
                    work[at_row(q), 128 * h:128 * h + 128] = rows[q][h]
            if s < 3:
                done = work[32 * s:32 * s + 32, :]
                change = product_tn(done[:, :128], done)
                work[32 * s + 32:, :] = work[32 * s + 32:, :] - change[32 * s + 32:, :]
        h = work[:, 128:]
        h_ref[at, :] = h
        diag[at, :] = jnp.where(upper, work[:, :128], 0.0).T
        m_ref[...] = m_ref[...] - product_tn(h, h)
        return carry

    lax.fori_loop(0, diag.shape[0] // 128, block, 0)


def window_kernel(part, lead, mine, beside, across, *refs):
    high_ref, low_ref, m_ref, diag, v_ref, h_ref, work = refs[-7:]
    first, size = PARTS[part]
    y = lax.rem(lax.axis_index("cand"), 4)
    for b, (own, other) in enumerate(((mine, beside), (beside, mine))):
        begin, end = max(first, W * b), min(first + size, W * b + W)
        if begin >= end:
            continue
        to = slice(begin - first, end - first)
        for n, holder in enumerate((own, other)):
            @pl.when(y == n)
            def _():
                v_ref[to, :] = holder[begin - W * b:end - W * b, :] * 0.0625

        @pl.when(y >= 2)
        def _():
            v_ref[to, :] = across[begin:end, :] * 0.0625

    if part:
        m_ref[...] = refs[0][...]
    else:
        square = lambda dim: lax.broadcasted_iota(jnp.int32, (RANK, RANK), dim)
        m_ref[...] = (square(0) == square(1)).astype(F32)
    unpack_tiles(lead[first // 32:(first + size) // 32, :], diag)
    factor_window(diag, v_ref, h_ref, m_ref, work)
    h = h_ref[...]
    high = h.astype(BF16)
    high_ref[...] = high
    low_ref[...] = (h - high.astype(F32)).astype(BF16)


def window_factor(part, lead, v, m):
    vmem = pl.BlockSpec(memory_space=pltpu.VMEM)
    size = PARTS[part][1]
    return pl.pallas_call(
        functools.partial(window_kernel, part),
        in_specs=[vmem] * (4 + len(m)),
        out_specs=[vmem] * 4,
        out_shape=[
            jax.ShapeDtypeStruct((size, RANK), BF16),
            jax.ShapeDtypeStruct((size, RANK), BF16),
            jax.ShapeDtypeStruct((RANK, RANK), F32),
            jax.ShapeDtypeStruct((size, 128), F32),
        ],
        scratch_shapes=[
            pltpu.VMEM((size, RANK), BF16),
            pltpu.VMEM((size, RANK), F32),
            pltpu.VMEM((128, 128 + RANK), F32),
        ],
        cost_estimate=pl.CostEstimate(flops=size * 10**7, bytes_accessed=size * 10**5, transcendentals=0),
        compiler_params=pltpu.CompilerParams(vmem_limit_bytes=32 * 2**20),
        name="window_factor",
    )(lead, *v, *m)


def rows_kernel(high0, low0, diag0, high1, low1, m_ref, diag1, kept, near, half, own, here, before, after, low, high, out, *scratch):
    own_diag, panel, blocks, sems = scratch
    cand = lax.axis_index("cand")
    x, y = cand // 4, lax.rem(cand, 4)
    v_own = own[...] * 0.0625
    split = PARTS[1][0]
    panel[:, :split] = dot_nt(v_own, high0[...]) + dot_nt(v_own, low0[...])
    panel[:, split:] = dot_nt(v_own, high1[...]) + dot_nt(v_own, low1[...])
    for n in range(2):
        @pl.when(cand == n)
        def _():
            row = lax.broadcasted_iota(jnp.int32, (W, WINDOW), 0) // 128 + 3 * n
            col = lax.broadcasted_iota(jnp.int32, (W, WINDOW), 1) // 128
            panel[...] = jnp.where(row > col, panel[...], 0.0)
            for a in range(3):
                at = W * n + 128 * a
                diag = diag0[at:at + 128, :] if at < split else diag1[at - split:at - split + 128, :]
                panel[128 * a:128 * a + 128, at:at + 128] = diag

    panel_copy = pltpu.make_async_copy(panel, out.at[0, :, pl.ds(0, WINDOW)], sems.at[16])
    panel_copy.start()
    unpack_tiles(kept[...] + near[...] + half[...], own_diag)
    m1, m2, m3 = split3(m_ref[...])
    q = (dot_nn(v_own, m1) + (dot_nn(v_own, m2) + dot_nn(v_own, m3))) * 0.0625
    q = jnp.where(cand < 2, 0.0, q)
    q1 = q.astype(BF16)
    q2 = (q - q1.astype(F32)).astype(BF16)
    stores = []
    for n, pieces in enumerate((here, before, after, (low, high))):
        column_y = lax.rem(y + (0, 3, 1, 2)[n], 4)
        for pair in range(2):
            v = pieces[pair][...] if n == 3 else pieces[2 * pair:2 * pair + 2]
            v = v.reshape(2 * W, RANK)
            slot = 2 * n + pair
            blocks[slot] = dot_nt(q1, v) + dot_nt(q2, v)
            if slot == 0:
                @pl.when(cand >= 2)
                def _():
                    for a in range(3):
                        at = slice(128 * a, 128 * a + 128)
                        blocks[0, at, at] += mirror(own_diag[at, :])

            for m in range(2):
                column = 4 * (x ^ ACROSS[2 * pair + m]) + column_y
                copy = pltpu.make_async_copy(
                    blocks.at[slot, :, pl.ds(W * m, W)],
                    out.at[0, :, pl.ds(pl.multiple_of(column * W, 128), W)],
                    sems.at[2 * slot + m],
                )
                stores.append((column, copy))

                @pl.when(column >= 2)
                def _():
                    copy.start()
    panel_copy.wait()
    for column, copy in stores:
        @pl.when(column >= 2)
        def _():
            copy.wait()


def factor_rows(*operands):
    vmem = pl.BlockSpec(memory_space=pltpu.VMEM)
    return pl.pallas_call(
        rows_kernel,
        in_specs=[vmem] * len(operands),
        out_specs=pl.BlockSpec(memory_space=pltpu.HBM),
        out_shape=jax.ShapeDtypeStruct((1, W, 16 * W), F32),
        scratch_shapes=[
            pltpu.VMEM((W, 128), F32),
            pltpu.VMEM((W, WINDOW), F32),
            pltpu.VMEM((8, W, 2 * W), F32),
            pltpu.SemaphoreType.DMA((17,)),
        ],
        compiler_params=pltpu.CompilerParams(vmem_limit_bytes=40 * 2**20),
        name="factor_rows",
    )(*operands)


def move_y(value, shift):
    return lax.ppermute(value, "cand", [(4 * x + y, 4 * x + (y + shift) % 4) for x in range(4) for y in range(4)])


def swap(value, bits):
    return lax.ppermute(value, "cand", [(i, i ^ bits) for i in range(16)])


def move_back(value, offset):
    return lax.ppermute(value, ("cand", "dom"), [(i, (i - offset) % 128) for i in range(128)])


def local(strain_ops, elem_scale, moduli, elem_block, elem_slot, mass, updates):
    cand = lax.axis_index("cand")
    x, y = cand // 4, cand % 4
    own = updates[0]

    small, row = 0.0, 0
    for part in (elem_scale, moduli, mass):
        rows, width = part.shape
        small = small + lax.pad(part, F32(0), ((row, 8 - row - rows, 0), (0, elem_scale.shape[1] - width, 0)))
        row += rows
    code = (elem_block[:, 0] * 16 + elem_slot)[None, :]
    strain = jnp.transpose(strain_ops, (1, 2, 0, 3))
    steps = strain.shape[3] // CHUNK

    beside = swap(own, 4)
    total = stiffness_tiles(0, steps // 2, strain, small, code, (), (BIN_ROWS,))
    total, beside = lax.optimization_barrier((total, beside))
    here = jnp.stack([own, beside])
    here = jnp.concatenate([here, swap(here, 12)])
    keep, far, two, three = stiffness_tiles(steps // 2, steps // 2, strain, small, code, total, (40, 40, 16, 16))

    far = move_back(far, 1)
    two = move_back(two, 2)
    three = move_back(three, 3)
    far, two, three, here = lax.optimization_barrier((far, two, three, here))
    kept = keep[:12] + far[:12] + two[:12] + three[:12]
    near = keep[12:24] + far[12:24]
    half = keep[24:36] + far[24:36]
    zero = jnp.zeros_like(kept)
    pick = lambda c: jnp.where(cand == c, kept, jnp.where(cand == c + 1, near, jnp.where(cand == c + 8, half, zero)))
    lead = jnp.concatenate([pick(0), pick(1)], axis=0)
    mine = functools.reduce(lambda u, n: jnp.where(x == ACROSS[n], here[n], u), range(1, 4), here[0])
    paired = swap(mine, 1)
    lead = lead + swap(lead, 4)
    lead = lead + swap(lead, 12)
    lead, paired, near, half = lax.optimization_barrier((lead, paired, near, half))
    near, half = move_back(near, 8), move_back(half, 64)
    across = swap(jnp.where(y == 0, jnp.concatenate([mine, paired]), jnp.concatenate([paired, mine])), 3)
    lead = lead + swap(lead, 1)
    lead = lead + swap(lead, 3)
    lead, across, here, near, half = lax.optimization_barrier((lead, across, here, near, half))

    before, after = move_y(here, 1), move_y(here, 3)
    window = (mine, paired, across)
    high0, low0, m, diag0 = window_factor(0, lead, window, ())
    m, before, after = lax.optimization_barrier((m, before, after))
    low, high = move_y(before[:2], 1), move_y(after[2:], 3)
    high1, low1, m, diag1 = window_factor(1, lead, window, (m,))
    return factor_rows(high0, low0, diag0, high1, low1, m, diag1, kept, near, half, own, here, before, after, low, high)


def solution(mesh):
    placed = (
        P(None, None, None, ("cand", "dom")),
        P(None, ("cand", "dom")),
        P(None, ("cand", "dom")),
        P(("cand", "dom"), None),
        P(("cand", "dom")),
        P("dom", "cand"),
        P("dom", "cand", None),
    )
    return jax.shard_map(
        local, mesh=mesh, in_specs=placed, out_specs=P("dom", "cand", None), check_vma=False
    )
```

```python
import functools

import jax
import jax.numpy as jnp
from jax import lax
from jax.experimental import pallas as pl
from jax.experimental.pallas import tpu as pltpu
from jax.sharding import PartitionSpec as P

F32 = jnp.float32
BF16 = jnp.bfloat16
W = 384
WINDOW = 768
PARTS = ((0, 512), (512, 256))
RANK = 256
SLOTS = 12
TILE = 512
CHUNK = 256
ACROSS = (0, 1, 3, 2)
BINS = {0: 0, 8: 12, 64: 24, 1: 40, 9: 52, 65: 64, 2: 80, 3: 96}
BIN_ROWS = 112


def split3(x):
    a = x.astype(BF16); r = x - a.astype(F32)
    b = r.astype(BF16); c = (r - b.astype(F32)).astype(BF16)
    return a, b, c


def dot_nn(a, b): return lax.dot_general(a, b, (((1,), (0,)), ((), ())), preferred_element_type=F32)
def dot_nt(a, b): return lax.dot_general(a, b, (((1,), (1,)), ((), ())), preferred_element_type=F32)


def six_terms(x1, x2, x3, axis):
    return jnp.concatenate([x1, x1, x2, x1, x2, x3], axis=axis)


def six_terms_across(y1, y2, y3, axis):
    return jnp.concatenate([y1, y2, y1, y3, y2, y1], axis=axis)


def product_tn(x, y):
    left, right = six_terms(*split3(x), 0), six_terms_across(*split3(y), 0)
    return lax.dot_general(left, right, (((0,), (0,)), ((), ())), preferred_element_type=F32)


def eliminate(rows, first):
    sub = lax.broadcasted_iota(jnp.int32, (8, 128), 0)
    n = len(rows)
    spread = lambda x, at: jnp.broadcast_to(x[at:at + 1, :], (8, 128))
    fetch = lambda k, q: jnp.broadcast_to(rows[q][0][:, first + k:first + k + 1], (8, 128))
    cols = {(q, k): fetch(k, q) for k in range(16) for q in range(k // 8, n)}
    for t in range(n):
        if 0 < t < n - 1:
            for k in range(8 * t + 8, 8 * t + 16):
                for q in range(t + 1, n):
                    cols[q, k] = fetch(k, q)
        for k in range(8 * t, 8 * t + 8):
            u = k % 8
            rs = lax.rsqrt(spread(cols[t, k], u))
            f = {q: cols[q, k] * rs for q in range(t, n)}
            for m in range(k + 1, min(8 * t + 16, 8 * n)):
                sm = spread(f[m // 8], m % 8)
                for q in range(m // 8, n):
                    cols[q, m] = cols[q, m] - f[q] * sm
            fm = jnp.where(sub > u, f[t], 0.0)
            for h in range(len(rows[t])):
                r = spread(rows[t][h], u) * rs
                rows[t][h] = jnp.where(sub == u, r, rows[t][h] - fm * r)
                for q in range(t + 1, n):
                    rows[q][h] = rows[q][h] - f[q] * r
    return rows


def unpack_tiles(packed, out_ref):
    n = packed.shape[0]
    lane = lax.broadcasted_iota(jnp.int32, (n, 128), 1)
    tile = lax.broadcasted_iota(jnp.int32, (n, 128), 0) % 4
    here = lane // 32 == tile
    entry = lane % 32
    for g in range(4):
        x = packed[:, 128 * g:128 * g + 128]
        turned = [x] + [pltpu.roll(x, 32 * r, 1) for r in range(1, 4)]
        for u in range(4):
            slot = turned[(0 - u) % 4]
            for v in range(1, 4):
                slot = jnp.where(tile == v, turned[(v - u) % 4], slot)
            p = 4 * g + u
            rows = ((30, 30), (31, 30)) if p == 15 else ((p, p), (29 - p, -1))
            for i, shift in rows:
                keep = here & (entry >= i) & (entry < (30 if i < 30 else i + 1))
                moved = pltpu.roll(slot, shift % 128, 1) if shift % 128 else slot
                out_ref[pl.ds(i, n, stride=32), :] = jnp.where(keep, moved, 0.0)


def stiffness_kernel(begin, strain, small, code, *refs):
    outs = refs[:-7] if begin == 0 else refs[1:-7]
    plain, weighted, sums, total, bins, data, sems = refs[-7:]
    steps = data.shape[0]
    copies = [
        pltpu.make_async_copy(strain.at[:, :, :, pl.ds((begin + n) * CHUNK, CHUNK)], data.at[n], sems.at[n])
        for n in range(steps)
    ]
    for copy in copies:
        copy.start()
    sums[...] = jnp.zeros_like(sums)
    if begin:
        total[...] = refs[0][...]
    else:
        total[...] = jnp.zeros_like(total)
        entry = lax.broadcasted_iota(jnp.int32, (W, TILE), 1)
        slot, at = entry // 32, entry % 32
        diagonal = jnp.where(slot == 15, 30 + at, jnp.where(at == 0, slot, jnp.where(at == 30 - slot, 29 - slot, -1)))
        spread = (diagonal == lax.broadcasted_iota(jnp.int32, (W, TILE), 0) % 32).astype(F32).astype(BF16)
        own = lax.broadcasted_iota(jnp.int32, (16, W), 1) // 32 == lax.broadcasted_iota(jnp.int32, (16, W), 0)
        mass = small[6:7, :W]
        total[:16, :] = sum(dot_nn(part, spread) for part in split3(jnp.where(own, mass, 0.0)))
    device = lax.axis_index("cand") * lax.axis_size("dom") + lax.axis_index("dom")
    offset = (device - code[...] // 16) & 127
    start = jnp.zeros_like(offset)
    for o, first in BINS.items():
        start = jnp.where(offset == o, first, start)
    bins[...] = start + code[...] % 16
    sub = lax.broadcasted_iota(jnp.int32, (8, 128), 0)

    def both(x):
        return jnp.concatenate([x[:, :128], x[:, 128:]], axis=0)

    def fold(a, b, bit):
        even = (sub & bit) == 0
        return jnp.where(even, a, pltpu.roll(b, bit, 0)) + jnp.where(even, pltpu.roll(a, 8 - bit, 0), b)

    def one_step(step, carry):
        for n, copy in enumerate(copies):
            @pl.when(step == n)
            def _():
                copy.wait()

        lanes = pl.ds(pl.multiple_of((begin + step) * CHUNK, CHUNK), CHUNK)
        weight = small[0:4, lanes]
        shear = both(weight * small[4:5, lanes])
        bulk = both(weight * small[5:6, lanes])
        for s in range(6):
            b = data[step, s].astype(F32)
            plain[s, :, 0:4, :] = b[:, :, :128]
            plain[s, :, 4:8, :] = b[:, :, 128:]
        for i in range(30):
            b = [plain[s, i] for s in range(6)]
            diverge = b[0] + b[1] + b[2]
            plain[6, i] = diverge
            weighted[6, i] = diverge * bulk
            for s in range(6):
                weighted[s, i] = b[s] * shear

        for first in range(0, 15, 2):
            slots = [p for p in (first, first + 1) if p < 15]
            owners = sorted({i for p in slots for i in (p, 29 - p)})
            rows = {i: [plain[s, i] for s in range(7)] for i in owners}
            ready = {(p, 31): None for p in slots}
            for col in range(first, 30):
                right = [weighted[s, col] for s in range(7)]
                for p in slots:
                    for i, l in ((p, col - p), (29 - p, col + 1)):
                        if col < i:
                            continue
                        products = [rows[i][s] * right[s] for s in range(7)]
                        value = products[0]
                        for product in products[1:]:
                            value = value + product
                        ready[p, l] = value
                        group = [(p, 8 * (l // 8) + m) for m in range(8)]
                        if not all(key in ready for key in group):
                            continue
                        eight = [ready.pop(key) for key in group]
                        eight = [jnp.zeros((8, 128), F32) if e is None else e for e in eight]
                        fours = []
                        for h in range(2):
                            a, b, c, d = eight[4 * h:4 * h + 4]
                            fours.append(fold(fold(a, b, 1), fold(c, d, 1), 2))
                        low, high = fours
                        r = 32 * p + 8 * (l // 8)
                        sums[r:r + 8, :128] = jnp.where(sub < 4, low, pltpu.roll(high, 4, 0))
                        sums[r:r + 8, 128:] = jnp.where(sub < 4, pltpu.roll(low, 4, 0), high)
        values = sums[...]
        high = values.astype(BF16)
        low = (values - high.astype(F32)).astype(BF16)
        chosen = lax.broadcasted_iota(jnp.int32, (BIN_ROWS, CHUNK), 0) == bins[:, lanes]
        chosen = chosen.astype(F32).astype(BF16)
        total[...] += dot_nt(chosen, high) + dot_nt(chosen, low)
        return carry

    lax.fori_loop(0, steps, one_step, 0)
    at = 0
    for out in outs:
        out[...] = total[at:at + out.shape[0], :]
        at += out.shape[0]


def stiffness_tiles(begin, steps, strain, small, code, total, outs):
    vmem = pl.BlockSpec(memory_space=pltpu.VMEM)
    return pl.pallas_call(
        functools.partial(stiffness_kernel, begin),
        in_specs=[pl.BlockSpec(memory_space=pltpu.HBM)] + [vmem] * (2 + len(total)),
        out_specs=[vmem] * len(outs),
        out_shape=[jax.ShapeDtypeStruct((r, TILE), F32) for r in outs],
        scratch_shapes=[
            pltpu.VMEM((7, 30, 8, 128), F32),
            pltpu.VMEM((7, 30, 8, 128), F32),
            pltpu.VMEM((TILE, CHUNK), F32),
            pltpu.VMEM((BIN_ROWS, TILE), F32),
            pltpu.VMEM(code.shape, jnp.int32),
            pltpu.VMEM((steps, 6, 30, 4, CHUNK), BF16),
            pltpu.SemaphoreType.DMA((steps,)),
        ],
        cost_estimate=pl.CostEstimate(flops=5 * 10**9, bytes_accessed=15 * 10**6, transcendentals=0),
        compiler_params=pltpu.CompilerParams(vmem_limit_bytes=32 * 2**20),
        name="stiffness_tiles",
    )(strain, small, code, *total)


def mirror(block):
    row = lax.broadcasted_iota(jnp.int32, block.shape, 0)
    col = lax.broadcasted_iota(jnp.int32, block.shape, 1)
    return jnp.where(row <= col, block, block.T)


def factor_window(diag, v_ref, h_ref, m_ref, work, ahead, last):
    square = lambda n, dim: lax.broadcasted_iota(jnp.int32, (n, n), dim)
    upper = square(128, 0) <= square(128, 1)
    blocks = diag.shape[0] // 128
    rows_of = lambda j: pl.ds(pl.multiple_of(j * 128, 128), 128)

    def start_block(at, m, to):
        v = v_ref[at, :]
        m1, m2, m3 = split3(m)
        p = dot_nn(v, m1) + (dot_nn(v, m2) + dot_nn(v, m3))
        p1, p2, p3 = split3(p)
        to[:, :128] = mirror(diag[at, :]) + (dot_nt(p1, v) + (dot_nt(p2, v) + dot_nt(p3, v)))
        to[:, 128:] = p

    def block(j, carry):
        at, following = rows_of(j), rows_of(jnp.minimum(j + 1, blocks - 1))
        done = last[...]
        m = m_ref[...] - product_tn(done, done)
        m_ref[...] = m
        start_block(following, m, ahead)
        for s in range(4):
            at_row = lambda q: slice(32 * s + 8 * q, 32 * s + 8 * q + 8)
            rows = [[work[at_row(q), 128 * h:128 * h + 128] for h in range(3)] for q in range(4)]
            rows = eliminate(rows, 32 * s)
            for q in range(4):
                for h in range(3):
                    work[at_row(q), 128 * h:128 * h + 128] = rows[q][h]
            if s < 3:
                later = 32 * s + 32
                done = work[32 * s:later, :]
                left = six_terms(*split3(done[:, :128]), 0).T[later:, :]
                work[later:, :] = work[later:, :] - dot_nn(left, six_terms_across(*split3(done), 0))
        h = work[:, 128:]
        h_ref[at, :] = h
        last[...] = h
        diag[at, :] = jnp.where(upper, work[:, :128], 0.0).T

        @pl.when(j < blocks - 1)
        def _():
            v = v_ref[following, :]
            h1, h2, h3 = split3(h)
            c = dot_nt(v, h1) + (dot_nt(v, h2) + dot_nt(v, h3))
            c = split3(c)
            left = six_terms(*c, 1)
            work[:, 128:] = ahead[:, 128:] - dot_nn(left, six_terms_across(h1, h2, h3, 0))
            work[:, :128] = ahead[:, :128] - dot_nt(left, six_terms_across(*c, 1))

        return carry

    last[...] = jnp.zeros_like(last)
    start_block(pl.ds(0, 128), m_ref[...], work)
    lax.fori_loop(0, blocks, block, 0)
    done = last[...]
    m_ref[...] = m_ref[...] - product_tn(done, done)


def window_kernel(part, lead, mine, beside, across, last_piece, *refs):
    high_ref, low_ref, m_ref, diag, v_ref, h_ref, work, ahead, last = refs[-9:]
    first, size = PARTS[part]
    y = lax.rem(lax.axis_index("cand"), 4)
    for b, holders in enumerate(((mine, beside, last_piece, across), (beside, mine, across, last_piece))):
        begin, end = max(first, W * b), min(first + size, W * b + W)
        if begin >= end:
            continue
        for n, holder in enumerate(holders):
            @pl.when(y == n)
            def _():
                v_ref[begin - first:end - first, :] = holder[begin - W * b:end - W * b, :] * 0.0625

    if part:
        m_ref[...] = refs[0][...]
    else:
        square = lambda dim: lax.broadcasted_iota(jnp.int32, (RANK, RANK), dim)
        m_ref[...] = (square(0) == square(1)).astype(F32)
    unpack_tiles(lead[first // 32:(first + size) // 32, :], diag)
    factor_window(diag, v_ref, h_ref, m_ref, work, ahead, last)
    h = h_ref[...]
    high = h.astype(BF16)
    high_ref[...] = high
    low_ref[...] = (h - high.astype(F32)).astype(BF16)


def window_factor(part, lead, v, m):
    vmem = pl.BlockSpec(memory_space=pltpu.VMEM)
    size = PARTS[part][1]
    return pl.pallas_call(
        functools.partial(window_kernel, part),
        in_specs=[vmem] * (5 + len(m)),
        out_specs=[vmem] * 4,
        out_shape=[
            jax.ShapeDtypeStruct((size, RANK), BF16),
            jax.ShapeDtypeStruct((size, RANK), BF16),
            jax.ShapeDtypeStruct((RANK, RANK), F32),
            jax.ShapeDtypeStruct((size, 128), F32),
        ],
        scratch_shapes=[
            pltpu.VMEM((size, RANK), BF16),
            pltpu.VMEM((size, RANK), F32),
            pltpu.VMEM((128, 128 + RANK), F32),
            pltpu.VMEM((128, 128 + RANK), F32),
            pltpu.VMEM((128, RANK), F32),
        ],
        cost_estimate=pl.CostEstimate(flops=size * 10**7, bytes_accessed=size * 10**5, transcendentals=0),
        compiler_params=pltpu.CompilerParams(vmem_limit_bytes=32 * 2**20),
        name="window_factor",
    )(lead, *v, *m)


def rows_kernel(high0, low0, diag0, high1, low1, m_ref, diag1, kept, near, half, own, here, before, after, low, high, out, *scratch):
    own_diag, panel, blocks, sems = scratch
    cand = lax.axis_index("cand")
    x, y = cand // 4, lax.rem(cand, 4)
    v_own = own[...] * 0.0625
    split = PARTS[1][0]
    panel[:, :split] = dot_nt(v_own, high0[...]) + dot_nt(v_own, low0[...])
    panel[:, split:] = dot_nt(v_own, high1[...]) + dot_nt(v_own, low1[...])
    for n in range(2):
        @pl.when(cand == n)
        def _():
            row = lax.broadcasted_iota(jnp.int32, (W, WINDOW), 0) // 128 + 3 * n
            col = lax.broadcasted_iota(jnp.int32, (W, WINDOW), 1) // 128
            panel[...] = jnp.where(row > col, panel[...], 0.0)
            for a in range(3):
                at = W * n + 128 * a
                diag = diag0[at:at + 128, :] if at < split else diag1[at - split:at - split + 128, :]
                panel[128 * a:128 * a + 128, at:at + 128] = diag

    panel_copy = pltpu.make_async_copy(panel, out.at[0, :, pl.ds(0, WINDOW)], sems.at[16])
    panel_copy.start()
    unpack_tiles(kept[...] + near[...] + half[...], own_diag)
    m1, m2, m3 = split3(m_ref[...])
    q = (dot_nn(v_own, m1) + (dot_nn(v_own, m2) + dot_nn(v_own, m3))) * 0.0625
    q = jnp.where(cand < 2, 0.0, q)
    q1 = q.astype(BF16)
    q2 = (q - q1.astype(F32)).astype(BF16)
    stores = []
    for n, pieces in enumerate((here, before, after, (low, high))):
        column_y = lax.rem(y + (0, 3, 1, 2)[n], 4)
        for pair in range(2):
            v = pieces[pair][...] if n == 3 else pieces[2 * pair:2 * pair + 2]
            v = v.reshape(2 * W, RANK)
            slot = 2 * n + pair
            blocks[slot] = dot_nt(q1, v) + dot_nt(q2, v)
            if slot == 0:
                @pl.when(cand >= 2)
                def _():
                    for a in range(3):
                        at = slice(128 * a, 128 * a + 128)
                        blocks[0, at, at] += mirror(own_diag[at, :])

            for m in range(2):
                column = 4 * (x ^ ACROSS[2 * pair + m]) + column_y
                copy = pltpu.make_async_copy(
                    blocks.at[slot, :, pl.ds(W * m, W)],
                    out.at[0, :, pl.ds(pl.multiple_of(column * W, 128), W)],
                    sems.at[2 * slot + m],
                )
                stores.append((column, copy))

                @pl.when(column >= 2)
                def _():
                    copy.start()
    panel_copy.wait()
    for column, copy in stores:
        @pl.when(column >= 2)
        def _():
            copy.wait()


def factor_rows(*operands):
    vmem = pl.BlockSpec(memory_space=pltpu.VMEM)
    return pl.pallas_call(
        rows_kernel,
        in_specs=[vmem] * len(operands),
        out_specs=pl.BlockSpec(memory_space=pltpu.HBM),
        out_shape=jax.ShapeDtypeStruct((1, W, 16 * W), F32),
        scratch_shapes=[
            pltpu.VMEM((W, 128), F32),
            pltpu.VMEM((W, WINDOW), F32),
            pltpu.VMEM((8, W, 2 * W), F32),
            pltpu.SemaphoreType.DMA((17,)),
        ],
        compiler_params=pltpu.CompilerParams(vmem_limit_bytes=40 * 2**20),
        name="factor_rows",
    )(*operands)


def move_y(value, shift):
    return lax.ppermute(value, "cand", [(4 * x + y, 4 * x + (y + shift) % 4) for x in range(4) for y in range(4)])


def swap(value, bits):
    return lax.ppermute(value, "cand", [(i, i ^ bits) for i in range(16)])


def move_back(value, offset):
    return lax.ppermute(value, ("cand", "dom"), [(i, (i - offset) % 128) for i in range(128)])


def local(strain_ops, elem_scale, moduli, elem_block, elem_slot, mass, updates):
    cand = lax.axis_index("cand")
    x, y = cand // 4, cand % 4
    own = updates[0]

    small, row = 0.0, 0
    for part in (elem_scale, moduli, mass):
        rows, width = part.shape
        small = small + lax.pad(part, F32(0), ((row, 8 - row - rows, 0), (0, elem_scale.shape[1] - width, 0)))
        row += rows
    code = elem_block.T * 16 + elem_slot[None, :]
    strain = jnp.transpose(strain_ops, (1, 2, 0, 3))
    steps = strain.shape[3] // CHUNK

    beside = swap(own, 4)
    total = stiffness_tiles(0, steps // 2, strain, small, code, (), (BIN_ROWS,))
    total, beside = lax.optimization_barrier((total, beside))
    here = jnp.stack([own, beside])
    here = jnp.concatenate([here, swap(here, 12)])
    keep, far, two, three = stiffness_tiles(steps // 2, steps // 2, strain, small, code, total, (40, 40, 16, 16))

    far = move_back(far, 1)
    two = move_back(two, 2)
    three = move_back(three, 3)
    far, two, three, here = lax.optimization_barrier((far, two, three, here))
    kept = keep[:12] + far[:12] + two[:12] + three[:12]
    near = keep[12:24] + far[12:24]
    half = keep[24:36] + far[24:36]
    zero = jnp.zeros_like(kept)
    pick = lambda c: jnp.where(cand == c, kept, jnp.where(cand == c + 1, near, jnp.where(cand == c + 8, half, zero)))
    lead = jnp.concatenate([pick(0), pick(1)], axis=0)
    mine = functools.reduce(lambda u, n: jnp.where(x == ACROSS[n], here[n], u), range(1, 4), here[0])
    paired, crossed = swap(mine, 1), swap(mine, 3)
    lead = lead + swap(lead, 4)
    lead = lead + swap(lead, 12)
    lead, paired, crossed, near, half = lax.optimization_barrier((lead, paired, crossed, near, half))
    near, half = move_back(near, 8), move_back(half, 64)
    last_piece = swap(crossed, 1)
    lead = lead + swap(lead, 1)
    lead = lead + swap(lead, 3)
    lead, last_piece, here = lax.optimization_barrier((lead, last_piece, here))

    before, after = move_y(here, 1), move_y(here, 3)
    window = (mine, paired, crossed, last_piece)
    high0, low0, m, diag0 = window_factor(0, lead, window, ())
    m, before, after, near, half = lax.optimization_barrier((m, before, after, near, half))
    low, high = move_y(before[:2], 1), move_y(after[2:], 3)
    high1, low1, m, diag1 = window_factor(1, lead, window, (m,))
    return factor_rows(high0, low0, diag0, high1, low1, m, diag1, kept, near, half, own, here, before, after, low, high)


def solution(mesh):
    placed = (
        P(None, None, None, ("cand", "dom")),
        P(None, ("cand", "dom")),
        P(None, ("cand", "dom")),
        P(("cand", "dom"), None),
        P(("cand", "dom")),
        P("dom", "cand"),
        P("dom", "cand", None),
    )
    return jax.shard_map(
        local, mesh=mesh, in_specs=placed, out_specs=P("dom", "cand", None), check_vma=False
    )
```

```python
import functools

import jax
import jax.numpy as jnp
from jax import lax
from jax.experimental import pallas as pl
from jax.experimental.pallas import tpu as pltpu
from jax.sharding import PartitionSpec as P

F32 = jnp.float32
BF16 = jnp.bfloat16
W = 384
WINDOW = 768
PARTS = ((0, 512), (512, 256))
RANK = 256
SLOTS = 12
TILE = 512
CHUNK = 256
ACROSS = (0, 1, 3, 2)
BINS = {0: 0, 8: 12, 64: 24, 1: 40, 9: 52, 65: 64, 2: 80, 3: 96}
BIN_ROWS = 112


def split3(x):
    a = x.astype(BF16); r = x - a.astype(F32)
    b = r.astype(BF16); c = (r - b.astype(F32)).astype(BF16)
    return a, b, c


def dot_nn(a, b): return lax.dot_general(a, b, (((1,), (0,)), ((), ())), preferred_element_type=F32)
def dot_nt(a, b): return lax.dot_general(a, b, (((1,), (1,)), ((), ())), preferred_element_type=F32)


def six_terms(x1, x2, x3, axis):
    return jnp.concatenate([x1, x1, x2, x1, x2, x3], axis=axis)


def six_terms_across(y1, y2, y3, axis):
    return jnp.concatenate([y1, y2, y1, y3, y2, y1], axis=axis)


def product_tn(x, y):
    left, right = six_terms(*split3(x), 0), six_terms_across(*split3(y), 0)
    return lax.dot_general(left, right, (((0,), (0,)), ((), ())), preferred_element_type=F32)


def eliminate(rows, first):
    sub = lax.broadcasted_iota(jnp.int32, (8, 128), 0)
    n = len(rows)
    spread = lambda x, at: jnp.broadcast_to(x[at:at + 1, :], (8, 128))
    fetch = lambda k, q: jnp.broadcast_to(rows[q][0][:, first + k:first + k + 1], (8, 128))
    cols = {(q, k): fetch(k, q) for k in range(16) for q in range(k // 8, n)}
    for t in range(n):
        if 0 < t < n - 1:
            for k in range(8 * t + 8, 8 * t + 16):
                for q in range(t + 1, n):
                    cols[q, k] = fetch(k, q)
        for k in range(8 * t, 8 * t + 8):
            u = k % 8
            rs = lax.rsqrt(spread(cols[t, k], u))
            f = {q: cols[q, k] * rs for q in range(t, n)}
            for m in range(k + 1, min(8 * t + 16, 8 * n)):
                sm = spread(f[m // 8], m % 8)
                for q in range(m // 8, n):
                    cols[q, m] = cols[q, m] - f[q] * sm
            fm = jnp.where(sub > u, f[t], 0.0)
            for h in range(len(rows[t])):
                r = spread(rows[t][h], u) * rs
                rows[t][h] = jnp.where(sub == u, r, rows[t][h] - fm * r)
                for q in range(t + 1, n):
                    rows[q][h] = rows[q][h] - f[q] * r
    return rows


def unpack_tiles(packed, out_ref):
    n = packed.shape[0]
    lane = lax.broadcasted_iota(jnp.int32, (n, 128), 1)
    tile = lax.broadcasted_iota(jnp.int32, (n, 128), 0) % 4
    here = lane // 32 == tile
    entry = lane % 32
    for g in range(4):
        x = packed[:, 128 * g:128 * g + 128]
        turned = [x] + [pltpu.roll(x, 32 * r, 1) for r in range(1, 4)]
        for u in range(4):
            slot = turned[(0 - u) % 4]
            for v in range(1, 4):
                slot = jnp.where(tile == v, turned[(v - u) % 4], slot)
            p = 4 * g + u
            rows = ((30, 30), (31, 30)) if p == 15 else ((p, p), (29 - p, -1))
            for i, shift in rows:
                keep = here & (entry >= i) & (entry < (30 if i < 30 else i + 1))
                moved = pltpu.roll(slot, shift % 128, 1) if shift % 128 else slot
                out_ref[pl.ds(i, n, stride=32), :] = jnp.where(keep, moved, 0.0)


def stiffness_kernel(begin, strain, small, code, *refs):
    outs = refs[:-7] if begin == 0 else refs[1:-7]
    plain, weighted, sums, total, bins, data, sems = refs[-7:]
    steps = data.shape[0]
    copies = [
        pltpu.make_async_copy(strain.at[:, :, :, pl.ds((begin + n) * CHUNK, CHUNK)], data.at[n], sems.at[n])
        for n in range(steps)
    ]
    for copy in copies:
        copy.start()
    sums[...] = jnp.zeros_like(sums)
    if begin:
        total[...] = refs[0][...]
    else:
        total[...] = jnp.zeros_like(total)
        entry = lax.broadcasted_iota(jnp.int32, (W, TILE), 1)
        slot, at = entry // 32, entry % 32
        diagonal = jnp.where(slot == 15, 30 + at, jnp.where(at == 0, slot, jnp.where(at == 30 - slot, 29 - slot, -1)))
        spread = (diagonal == lax.broadcasted_iota(jnp.int32, (W, TILE), 0) % 32).astype(F32).astype(BF16)
        own = lax.broadcasted_iota(jnp.int32, (16, W), 1) // 32 == lax.broadcasted_iota(jnp.int32, (16, W), 0)
        mass = small[6:7, :W]
        total[:16, :] = sum(dot_nn(part, spread) for part in split3(jnp.where(own, mass, 0.0)))
    device = lax.axis_index("cand") * lax.axis_size("dom") + lax.axis_index("dom")
    offset = (device - code[...] // 16) & 127
    start = jnp.zeros_like(offset)
    for o, first in BINS.items():
        start = jnp.where(offset == o, first, start)
    bins[...] = start + code[...] % 16
    sub = lax.broadcasted_iota(jnp.int32, (8, 128), 0)

    def both(x):
        return jnp.concatenate([x[:, :128], x[:, 128:]], axis=0)

    def fold(a, b, bit):
        even = (sub & bit) == 0
        return jnp.where(even, a, pltpu.roll(b, bit, 0)) + jnp.where(even, pltpu.roll(a, 8 - bit, 0), b)

    def one_step(step, carry):
        for n, copy in enumerate(copies):
            @pl.when(step == n)
            def _():
                copy.wait()

        lanes = pl.ds(pl.multiple_of((begin + step) * CHUNK, CHUNK), CHUNK)
        weight = small[0:4, lanes]
        shear = both(weight * small[4:5, lanes])
        bulk = both(weight * small[5:6, lanes])
        for s in range(6):
            b = data[step, s].astype(F32)
            plain[s, :, 0:4, :] = b[:, :, :128]
            plain[s, :, 4:8, :] = b[:, :, 128:]
        for i in range(30):
            b = [plain[s, i] for s in range(6)]
            diverge = b[0] + b[1] + b[2]
            plain[6, i] = diverge
            weighted[6, i] = diverge * bulk
            for s in range(6):
                weighted[s, i] = b[s] * shear

        for first in range(0, 15, 2):
            slots = [p for p in (first, first + 1) if p < 15]
            owners = sorted({i for p in slots for i in (p, 29 - p)})
            rows = {i: [plain[s, i] for s in range(7)] for i in owners}
            ready = {(p, 31): None for p in slots}
            for col in range(first, 30):
                right = [weighted[s, col] for s in range(7)]
                for p in slots:
                    for i, l in ((p, col - p), (29 - p, col + 1)):
                        if col < i:
                            continue
                        products = [rows[i][s] * right[s] for s in range(7)]
                        value = products[0]
                        for product in products[1:]:
                            value = value + product
                        ready[p, l] = value
                        group = [(p, 8 * (l // 8) + m) for m in range(8)]
                        if not all(key in ready for key in group):
                            continue
                        eight = [ready.pop(key) for key in group]
                        eight = [jnp.zeros((8, 128), F32) if e is None else e for e in eight]
                        fours = []
                        for h in range(2):
                            a, b, c, d = eight[4 * h:4 * h + 4]
                            fours.append(fold(fold(a, b, 1), fold(c, d, 1), 2))
                        low, high = fours
                        r = 32 * p + 8 * (l // 8)
                        sums[r:r + 8, :128] = jnp.where(sub < 4, low, pltpu.roll(high, 4, 0))
                        sums[r:r + 8, 128:] = jnp.where(sub < 4, pltpu.roll(low, 4, 0), high)
        values = sums[...]
        high = values.astype(BF16)
        low = (values - high.astype(F32)).astype(BF16)
        chosen = lax.broadcasted_iota(jnp.int32, (BIN_ROWS, CHUNK), 0) == bins[:, lanes]
        chosen = chosen.astype(F32).astype(BF16)
        total[...] += dot_nt(chosen, high) + dot_nt(chosen, low)
        return carry

    lax.fori_loop(0, steps, one_step, 0)
    at = 0
    for out in outs:
        out[...] = total[at:at + out.shape[0], :]
        at += out.shape[0]


def stiffness_tiles(begin, steps, strain, small, code, total, outs):
    vmem = pl.BlockSpec(memory_space=pltpu.VMEM)
    return pl.pallas_call(
        functools.partial(stiffness_kernel, begin),
        in_specs=[pl.BlockSpec(memory_space=pltpu.HBM)] + [vmem] * (2 + len(total)),
        out_specs=[vmem] * len(outs),
        out_shape=[jax.ShapeDtypeStruct((r, TILE), F32) for r in outs],
        scratch_shapes=[
            pltpu.VMEM((7, 30, 8, 128), F32),
            pltpu.VMEM((7, 30, 8, 128), F32),
            pltpu.VMEM((TILE, CHUNK), F32),
            pltpu.VMEM((BIN_ROWS, TILE), F32),
            pltpu.VMEM(code.shape, jnp.int32),
            pltpu.VMEM((steps, 6, 30, 4, CHUNK), BF16),
            pltpu.SemaphoreType.DMA((steps,)),
        ],
        cost_estimate=pl.CostEstimate(flops=5 * 10**9, bytes_accessed=15 * 10**6, transcendentals=0),
        compiler_params=pltpu.CompilerParams(vmem_limit_bytes=32 * 2**20),
        name="stiffness_tiles",
    )(strain, small, code, *total)


def mirror(block):
    row = lax.broadcasted_iota(jnp.int32, block.shape, 0)
    col = lax.broadcasted_iota(jnp.int32, block.shape, 1)
    return jnp.where(row <= col, block, block.T)


def factor_window(diag, v_ref, h_ref, m_ref, work, ahead, last):
    square = lambda n, dim: lax.broadcasted_iota(jnp.int32, (n, n), dim)
    upper = square(128, 0) <= square(128, 1)
    blocks = diag.shape[0] // 128
    rows_of = lambda j: pl.ds(pl.multiple_of(j * 128, 128), 128)

    def start_block(at, m, to):
        v = v_ref[at, :]
        m1, m2, m3 = split3(m)
        p = dot_nn(v, m1) + (dot_nn(v, m2) + dot_nn(v, m3))
        p1, p2, p3 = split3(p)
        to[:, :128] = mirror(diag[at, :]) + (dot_nt(p1, v) + (dot_nt(p2, v) + dot_nt(p3, v)))
        to[:, 128:] = p

    def block(j, carry):
        at, following = rows_of(j), rows_of(jnp.minimum(j + 1, blocks - 1))
        done = last[...]
        m = m_ref[...] - product_tn(done, done)
        m_ref[...] = m
        start_block(following, m, ahead)
        for s in range(4):
            at_row = lambda q: slice(32 * s + 8 * q, 32 * s + 8 * q + 8)
            rows = [[work[at_row(q), 128 * h:128 * h + 128] for h in range(3)] for q in range(4)]
            rows = eliminate(rows, 32 * s)
            for q in range(4):
                for h in range(3):
                    work[at_row(q), 128 * h:128 * h + 128] = rows[q][h]
            if s < 3:
                later = 32 * s + 32
                done = work[32 * s:later, :]
                left = six_terms(*split3(done[:, :128]), 0).T[later:, :]
                work[later:, :] = work[later:, :] - dot_nn(left, six_terms_across(*split3(done), 0))
        h = work[:, 128:]
        h_ref[at, :] = h
        last[...] = h
        diag[at, :] = jnp.where(upper, work[:, :128], 0.0).T

        @pl.when(j < blocks - 1)
        def _():
            v = v_ref[following, :]
            h1, h2, h3 = split3(h)
            c = dot_nt(v, h1) + (dot_nt(v, h2) + dot_nt(v, h3))
            c = split3(c)
            left = six_terms(*c, 1)
            work[:, 128:] = ahead[:, 128:] - dot_nn(left, six_terms_across(h1, h2, h3, 0))
            work[:, :128] = ahead[:, :128] - dot_nt(left, six_terms_across(*c, 1))

        return carry

    last[...] = jnp.zeros_like(last)
    start_block(pl.ds(0, 128), m_ref[...], work)
    lax.fori_loop(0, blocks, block, 0)
    done = last[...]
    m_ref[...] = m_ref[...] - product_tn(done, done)


def window_kernel(part, lead, mine, beside, across, last_piece, *refs):
    high_ref, low_ref, m_ref, diag, v_ref, h_ref, work, ahead, last = refs[-9:]
    first, size = PARTS[part]
    y = lax.rem(lax.axis_index("cand"), 4)
    for b, holders in enumerate(((mine, beside, last_piece, across), (beside, mine, across, last_piece))):
        begin, end = max(first, W * b), min(first + size, W * b + W)
        if begin >= end:
            continue
        for n, holder in enumerate(holders):
            @pl.when(y == n)
            def _():
                v_ref[begin - first:end - first, :] = holder[begin - W * b:end - W * b, :] * 0.0625

    if part:
        m_ref[...] = refs[0][...]
    else:
        square = lambda dim: lax.broadcasted_iota(jnp.int32, (RANK, RANK), dim)
        m_ref[...] = (square(0) == square(1)).astype(F32)
    unpack_tiles(lead[first // 32:(first + size) // 32, :], diag)
    factor_window(diag, v_ref, h_ref, m_ref, work, ahead, last)
    h = h_ref[...]
    high = h.astype(BF16)
    high_ref[...] = high
    low_ref[...] = (h - high.astype(F32)).astype(BF16)


def window_factor(part, lead, v, m):
    vmem = pl.BlockSpec(memory_space=pltpu.VMEM)
    size = PARTS[part][1]
    return pl.pallas_call(
        functools.partial(window_kernel, part),
        in_specs=[vmem] * (5 + len(m)),
        out_specs=[vmem] * 4,
        out_shape=[
            jax.ShapeDtypeStruct((size, RANK), BF16),
            jax.ShapeDtypeStruct((size, RANK), BF16),
            jax.ShapeDtypeStruct((RANK, RANK), F32),
            jax.ShapeDtypeStruct((size, 128), F32),
        ],
        scratch_shapes=[
            pltpu.VMEM((size, RANK), BF16),
            pltpu.VMEM((size, RANK), F32),
            pltpu.VMEM((128, 128 + RANK), F32),
            pltpu.VMEM((128, 128 + RANK), F32),
            pltpu.VMEM((128, RANK), F32),
        ],
        cost_estimate=pl.CostEstimate(flops=size * 10**7, bytes_accessed=size * 10**5, transcendentals=0),
        compiler_params=pltpu.CompilerParams(vmem_limit_bytes=32 * 2**20),
        name="window_factor",
    )(lead, *v, *m)


def rows_kernel(high0, low0, diag0, high1, low1, m_ref, diag1, kept, near, half, own, here, before, after, low, high, out, *scratch):
    own_diag, panel, blocks, sems = scratch
    cand = lax.axis_index("cand")
    x, y = cand // 4, lax.rem(cand, 4)
    v_own = own[...] * 0.0625
    split = PARTS[1][0]
    panel[:, :split] = dot_nt(v_own, high0[...]) + dot_nt(v_own, low0[...])
    panel[:, split:] = dot_nt(v_own, high1[...]) + dot_nt(v_own, low1[...])
    for n in range(2):
        @pl.when(cand == n)
        def _():
            row = lax.broadcasted_iota(jnp.int32, (W, WINDOW), 0) // 128 + 3 * n
            col = lax.broadcasted_iota(jnp.int32, (W, WINDOW), 1) // 128
            panel[...] = jnp.where(row > col, panel[...], 0.0)
            for a in range(3):
                at = W * n + 128 * a
                diag = diag0[at:at + 128, :] if at < split else diag1[at - split:at - split + 128, :]
                panel[128 * a:128 * a + 128, at:at + 128] = diag

    panel_copy = pltpu.make_async_copy(panel, out.at[0, :, pl.ds(0, WINDOW)], sems.at[16])
    panel_copy.start()
    unpack_tiles(kept[...] + near[...] + half[...], own_diag)
    m1, m2, m3 = split3(m_ref[...])
    q = (dot_nn(v_own, m1) + (dot_nn(v_own, m2) + dot_nn(v_own, m3))) * 0.0625
    q = jnp.where(cand < 2, 0.0, q)
    q1 = q.astype(BF16)
    q2 = (q - q1.astype(F32)).astype(BF16)
    stores = []
    for n, pieces in enumerate((here, before, after, (low, high))):
        column_y = lax.rem(y + (0, 3, 1, 2)[n], 4)
        for pair in range(2):
            v = pieces[pair][...] if n == 3 else pieces[2 * pair:2 * pair + 2]
            v = v.reshape(2 * W, RANK)
            slot = 2 * n + pair
            blocks[slot] = dot_nt(q1, v) + dot_nt(q2, v)
            if slot == 0:
                @pl.when(cand >= 2)
                def _():
                    for a in range(3):
                        at = slice(128 * a, 128 * a + 128)
                        blocks[0, at, at] += mirror(own_diag[at, :])

            for m in range(2):
                column = 4 * (x ^ ACROSS[2 * pair + m]) + column_y
                copy = pltpu.make_async_copy(
                    blocks.at[slot, :, pl.ds(W * m, W)],
                    out.at[0, :, pl.ds(pl.multiple_of(column * W, 128), W)],
                    sems.at[2 * slot + m],
                )
                stores.append((column, copy))

                @pl.when(column >= 2)
                def _():
                    copy.start()
    panel_copy.wait()
    for column, copy in stores:
        @pl.when(column >= 2)
        def _():
            copy.wait()


def factor_rows(*operands):
    vmem = pl.BlockSpec(memory_space=pltpu.VMEM)
    return pl.pallas_call(
        rows_kernel,
        in_specs=[vmem] * len(operands),
        out_specs=pl.BlockSpec(memory_space=pltpu.HBM),
        out_shape=jax.ShapeDtypeStruct((1, W, 16 * W), F32),
        scratch_shapes=[
            pltpu.VMEM((W, 128), F32),
            pltpu.VMEM((W, WINDOW), F32),
            pltpu.VMEM((8, W, 2 * W), F32),
            pltpu.SemaphoreType.DMA((17,)),
        ],
        compiler_params=pltpu.CompilerParams(vmem_limit_bytes=40 * 2**20),
        name="factor_rows",
    )(*operands)


def move_y(value, shift):
    return lax.ppermute(value, "cand", [(4 * x + y, 4 * x + (y + shift) % 4) for x in range(4) for y in range(4)])


def swap(value, bits):
    return lax.ppermute(value, "cand", [(i, i ^ bits) for i in range(16)])


def move_back(value, offset):
    return lax.ppermute(value, ("cand", "dom"), [(i, (i - offset) % 128) for i in range(128)])


def local(strain_ops, elem_scale, moduli, elem_block, elem_slot, mass, updates):
    cand = lax.axis_index("cand")
    x, y = cand // 4, cand % 4
    own = updates[0]

    small, row = 0.0, 0
    for part in (elem_scale, moduli, mass):
        rows, width = part.shape
        small = small + lax.pad(part, F32(0), ((row, 8 - row - rows, 0), (0, elem_scale.shape[1] - width, 0)))
        row += rows
    code = elem_block.T * 16 + elem_slot[None, :]
    strain = jnp.transpose(strain_ops, (1, 2, 0, 3))
    steps = strain.shape[3] // CHUNK

    beside = swap(own, 4)
    total = stiffness_tiles(0, steps // 2, strain, small, code, (), (BIN_ROWS,))
    total, beside = lax.optimization_barrier((total, beside))
    here = jnp.stack([own, beside])
    here = jnp.concatenate([here, swap(here, 12)])
    keep, far, two, three = stiffness_tiles(steps // 2, steps // 2, strain, small, code, total, (40, 40, 16, 16))

    far = move_back(far, 1)
    two = move_back(two, 2)
    three = move_back(three, 3)
    far, two, three, here = lax.optimization_barrier((far, two, three, here))
    kept = keep[:12] + far[:12] + two[:12] + three[:12]
    near = keep[12:24] + far[12:24]
    half = keep[24:36] + far[24:36]
    zero = jnp.zeros_like(kept)
    pick = lambda c: jnp.where(cand == c, kept, jnp.where(cand == c + 1, near, jnp.where(cand == c + 8, half, zero)))
    lead = jnp.concatenate([pick(0), pick(1)], axis=0)
    mine = functools.reduce(lambda u, n: jnp.where(x == ACROSS[n], here[n], u), range(1, 4), here[0])
    paired, crossed = swap(mine, 1), swap(mine, 3)
    lead = lead + swap(lead, 4)
    lead = lead + swap(lead, 12)
    lead, paired, crossed, near, half = lax.optimization_barrier((lead, paired, crossed, near, half))
    near, half = move_back(near, 8), move_back(half, 64)
    last_piece = swap(crossed, 1)
    lead = lead + swap(lead, 3)
    lead = lead + swap(lead, 1)
    lead, last_piece, here = lax.optimization_barrier((lead, last_piece, here))

    before, after = move_y(here, 1), move_y(here, 3)
    window = (mine, paired, crossed, last_piece)
    high0, low0, m, diag0 = window_factor(0, lead, window, ())
    m, before, after, near, half = lax.optimization_barrier((m, before, after, near, half))
    low, high = move_y(before[:2], 1), move_y(after[2:], 3)
    high1, low1, m, diag1 = window_factor(1, lead, window, (m,))
    return factor_rows(high0, low0, diag0, high1, low1, m, diag1, kept, near, half, own, here, before, after, low, high)


def solution(mesh):
    placed = (
        P(None, None, None, ("cand", "dom")),
        P(None, ("cand", "dom")),
        P(None, ("cand", "dom")),
        P(("cand", "dom"), None),
        P(("cand", "dom")),
        P("dom", "cand"),
        P("dom", "cand", None),
    )
    return jax.shard_map(
        local, mesh=mesh, in_specs=placed, out_specs=P("dom", "cand", None), check_vma=False
    )
```

```python
import functools

import jax
import jax.numpy as jnp
from jax import lax
from jax.experimental import pallas as pl
from jax.experimental.pallas import tpu as pltpu
from jax.sharding import PartitionSpec as P

F32 = jnp.float32
BF16 = jnp.bfloat16
W = 384
WINDOW = 768
PARTS = ((0, 512), (512, 256))
RANK = 256
SLOTS = 12
TILE = 512
CHUNK = 256
ACROSS = (0, 1, 3, 2)
BINS = {0: 0, 8: 12, 64: 24, 1: 40, 9: 52, 65: 64, 2: 80, 3: 96}
BIN_ROWS = 112


def split3(x):
    a = x.astype(BF16); r = x - a.astype(F32)
    b = r.astype(BF16); c = (r - b.astype(F32)).astype(BF16)
    return a, b, c


def dot_nn(a, b): return lax.dot_general(a, b, (((1,), (0,)), ((), ())), preferred_element_type=F32)
def dot_nt(a, b): return lax.dot_general(a, b, (((1,), (1,)), ((), ())), preferred_element_type=F32)


def six_terms(x1, x2, x3, axis):
    return jnp.concatenate([x1, x1, x2, x1, x2, x3], axis=axis)


def six_terms_across(y1, y2, y3, axis):
    return jnp.concatenate([y1, y2, y1, y3, y2, y1], axis=axis)


def product_tn(x, y):
    left, right = six_terms(*split3(x), 0), six_terms_across(*split3(y), 0)
    return lax.dot_general(left, right, (((0,), (0,)), ((), ())), preferred_element_type=F32)


def eliminate(rows, first):
    sub = lax.broadcasted_iota(jnp.int32, (8, 128), 0)
    n = len(rows)
    spread = lambda x, at: jnp.broadcast_to(x[at:at + 1, :], (8, 128))
    fetch = lambda k, q: jnp.broadcast_to(rows[q][0][:, first + k:first + k + 1], (8, 128))
    cols = {(q, k): fetch(k, q) for k in range(16) for q in range(k // 8, n)}
    for t in range(n):
        if 0 < t < n - 1:
            for k in range(8 * t + 8, 8 * t + 16):
                for q in range(t + 1, n):
                    cols[q, k] = fetch(k, q)
        for k in range(8 * t, 8 * t + 8):
            u = k % 8
            rs = lax.rsqrt(spread(cols[t, k], u))
            f = {q: cols[q, k] * rs for q in range(t, n)}
            for m in range(k + 1, min(8 * t + 16, 8 * n)):
                sm = spread(f[m // 8], m % 8)
                for q in range(m // 8, n):
                    cols[q, m] = cols[q, m] - f[q] * sm
            fm = jnp.where(sub > u, f[t], 0.0)
            for h in range(len(rows[t])):
                r = spread(rows[t][h], u) * rs
                rows[t][h] = jnp.where(sub == u, r, rows[t][h] - fm * r)
                for q in range(t + 1, n):
                    rows[q][h] = rows[q][h] - f[q] * r
    return rows


def unpack_tiles(packed, out_ref):
    n = packed.shape[0]
    lane = lax.broadcasted_iota(jnp.int32, (n, 128), 1)
    tile = lax.broadcasted_iota(jnp.int32, (n, 128), 0) % 4
    here = lane // 32 == tile
    entry = lane % 32
    for g in range(4):
        x = packed[:, 128 * g:128 * g + 128]
        turned = [x] + [pltpu.roll(x, 32 * r, 1) for r in range(1, 4)]
        for u in range(4):
            slot = turned[(0 - u) % 4]
            for v in range(1, 4):
                slot = jnp.where(tile == v, turned[(v - u) % 4], slot)
            p = 4 * g + u
            rows = ((30, 30), (31, 30)) if p == 15 else ((p, p), (29 - p, -1))
            for i, shift in rows:
                keep = here & (entry >= i) & (entry < (30 if i < 30 else i + 1))
                moved = pltpu.roll(slot, shift % 128, 1) if shift % 128 else slot
                out_ref[pl.ds(i, n, stride=32), :] = jnp.where(keep, moved, 0.0)


def stiffness_kernel(begin, strain, small, code, *refs):
    outs = refs[:-7] if begin == 0 else refs[1:-7]
    plain, weighted, sums, total, bins, data, sems = refs[-7:]
    steps = data.shape[0]
    copies = [
        pltpu.make_async_copy(strain.at[:, :, :, pl.ds((begin + n) * CHUNK, CHUNK)], data.at[n], sems.at[n])
        for n in range(steps)
    ]
    for copy in copies:
        copy.start()
    sums[...] = jnp.zeros_like(sums)
    if begin:
        total[...] = refs[0][...]
    else:
        total[...] = jnp.zeros_like(total)
        entry = lax.broadcasted_iota(jnp.int32, (W, TILE), 1)
        slot, at = entry // 32, entry % 32
        diagonal = jnp.where(slot == 15, 30 + at, jnp.where(at == 0, slot, jnp.where(at == 30 - slot, 29 - slot, -1)))
        spread = (diagonal == lax.broadcasted_iota(jnp.int32, (W, TILE), 0) % 32).astype(F32).astype(BF16)
        own = lax.broadcasted_iota(jnp.int32, (16, W), 1) // 32 == lax.broadcasted_iota(jnp.int32, (16, W), 0)
        mass = small[6:7, :W]
        total[:16, :] = sum(dot_nn(part, spread) for part in split3(jnp.where(own, mass, 0.0)))
    device = lax.axis_index("cand") * lax.axis_size("dom") + lax.axis_index("dom")
    offset = (device - code[...] // 16) & 127
    start = jnp.zeros_like(offset)
    for o, first in BINS.items():
        start = jnp.where(offset == o, first, start)
    bins[...] = start + code[...] % 16
    sub = lax.broadcasted_iota(jnp.int32, (8, 128), 0)

    def both(x):
        return jnp.concatenate([x[:, :128], x[:, 128:]], axis=0)

    def fold(a, b, bit):
        even = (sub & bit) == 0
        return jnp.where(even, a, pltpu.roll(b, bit, 0)) + jnp.where(even, pltpu.roll(a, 8 - bit, 0), b)

    def one_step(step, carry):
        for n, copy in enumerate(copies):
            @pl.when(step == n)
            def _():
                copy.wait()

        lanes = pl.ds(pl.multiple_of((begin + step) * CHUNK, CHUNK), CHUNK)
        weight = small[0:4, lanes]
        shear = both(weight * small[4:5, lanes])
        bulk = both(weight * small[5:6, lanes])
        for s in range(6):
            b = data[step, s].astype(F32)
            plain[s, :, 0:4, :] = b[:, :, :128]
            plain[s, :, 4:8, :] = b[:, :, 128:]
        for i in range(30):
            b = [plain[s, i] for s in range(6)]
            diverge = b[0] + b[1] + b[2]
            plain[6, i] = diverge
            weighted[6, i] = diverge * bulk
            for s in range(6):
                weighted[s, i] = b[s] * shear

        for first in range(0, 15, 2):
            slots = [p for p in (first, first + 1) if p < 15]
            owners = sorted({i for p in slots for i in (p, 29 - p)})
            rows = {i: [plain[s, i] for s in range(7)] for i in owners}
            ready = {(p, 31): None for p in slots}
            for col in range(first, 30):
                right = [weighted[s, col] for s in range(7)]
                for p in slots:
                    for i, l in ((p, col - p), (29 - p, col + 1)):
                        if col < i:
                            continue
                        products = [rows[i][s] * right[s] for s in range(7)]
                        value = products[0]
                        for product in products[1:]:
                            value = value + product
                        ready[p, l] = value
                        group = [(p, 8 * (l // 8) + m) for m in range(8)]
                        if not all(key in ready for key in group):
                            continue
                        eight = [ready.pop(key) for key in group]
                        eight = [jnp.zeros((8, 128), F32) if e is None else e for e in eight]
                        fours = []
                        for h in range(2):
                            a, b, c, d = eight[4 * h:4 * h + 4]
                            fours.append(fold(fold(a, b, 1), fold(c, d, 1), 2))
                        low, high = fours
                        r = 32 * p + 8 * (l // 8)
                        sums[r:r + 8, :128] = jnp.where(sub < 4, low, pltpu.roll(high, 4, 0))
                        sums[r:r + 8, 128:] = jnp.where(sub < 4, pltpu.roll(low, 4, 0), high)
        values = sums[...]
        high = values.astype(BF16)
        low = (values - high.astype(F32)).astype(BF16)
        chosen = lax.broadcasted_iota(jnp.int32, (BIN_ROWS, CHUNK), 0) == bins[:, lanes]
        chosen = chosen.astype(F32).astype(BF16)
        total[...] += dot_nt(chosen, high) + dot_nt(chosen, low)
        return carry

    lax.fori_loop(0, steps, one_step, 0)
    at = 0
    for out in outs:
        out[...] = total[at:at + out.shape[0], :]
        at += out.shape[0]


def stiffness_tiles(begin, steps, strain, small, code, total, outs):
    vmem = pl.BlockSpec(memory_space=pltpu.VMEM)
    return pl.pallas_call(
        functools.partial(stiffness_kernel, begin),
        in_specs=[pl.BlockSpec(memory_space=pltpu.HBM)] + [vmem] * (2 + len(total)),
        out_specs=[vmem] * len(outs),
        out_shape=[jax.ShapeDtypeStruct((r, TILE), F32) for r in outs],
        scratch_shapes=[
            pltpu.VMEM((7, 30, 8, 128), F32),
            pltpu.VMEM((7, 30, 8, 128), F32),
            pltpu.VMEM((TILE, CHUNK), F32),
            pltpu.VMEM((BIN_ROWS, TILE), F32),
            pltpu.VMEM(code.shape, jnp.int32),
            pltpu.VMEM((steps, 6, 30, 4, CHUNK), BF16),
            pltpu.SemaphoreType.DMA((steps,)),
        ],
        cost_estimate=pl.CostEstimate(flops=5 * 10**9, bytes_accessed=15 * 10**6, transcendentals=0),
        compiler_params=pltpu.CompilerParams(vmem_limit_bytes=32 * 2**20),
        name="stiffness_tiles",
    )(strain, small, code, *total)


def mirror(block):
    row = lax.broadcasted_iota(jnp.int32, block.shape, 0)
    col = lax.broadcasted_iota(jnp.int32, block.shape, 1)
    return jnp.where(row <= col, block, block.T)


def factor_window(diag, v_ref, h_ref, m_ref, work, ahead, last):
    square = lambda n, dim: lax.broadcasted_iota(jnp.int32, (n, n), dim)
    upper = square(128, 0) <= square(128, 1)
    blocks = diag.shape[0] // 128
    rows_of = lambda j: pl.ds(pl.multiple_of(j * 128, 128), 128)

    def start_block(at, m, to):
        v = v_ref[at, :]
        m1, m2, m3 = split3(m)
        p = dot_nn(v, m1) + (dot_nn(v, m2) + dot_nn(v, m3))
        p1, p2, p3 = split3(p)
        to[:, :128] = mirror(diag[at, :]) + (dot_nt(p1, v) + (dot_nt(p2, v) + dot_nt(p3, v)))
        to[:, 128:] = p

    def block(j, carry):
        at, following = rows_of(j), rows_of(jnp.minimum(j + 1, blocks - 1))
        done = last[...]
        m = m_ref[...] - product_tn(done, done)
        m_ref[...] = m
        start_block(following, m, ahead)
        for s in range(4):
            at_row = lambda q: slice(32 * s + 8 * q, 32 * s + 8 * q + 8)
            rows = [[work[at_row(q), 128 * h:128 * h + 128] for h in range(3)] for q in range(4)]
            rows = eliminate(rows, 32 * s)
            for q in range(4):
                for h in range(3):
                    work[at_row(q), 128 * h:128 * h + 128] = rows[q][h]
            if s < 3:
                later = 32 * s + 32
                done = work[32 * s:later, :]
                left = six_terms(*split3(done[:, :128]), 0).T[later:, :]
                work[later:, :] = work[later:, :] - dot_nn(left, six_terms_across(*split3(done), 0))
        h = work[:, 128:]
        h_ref[at, :] = h
        last[...] = h
        diag[at, :] = jnp.where(upper, work[:, :128], 0.0).T

        @pl.when(j < blocks - 1)
        def _():
            v = v_ref[following, :]
            h1, h2, h3 = split3(h)
            c = dot_nt(v, h1) + (dot_nt(v, h2) + dot_nt(v, h3))
            c = split3(c)
            left = six_terms(*c, 1)
            work[:, 128:] = ahead[:, 128:] - dot_nn(left, six_terms_across(h1, h2, h3, 0))
            work[:, :128] = ahead[:, :128] - dot_nt(left, six_terms_across(*c, 1))

        return carry

    last[...] = jnp.zeros_like(last)
    start_block(pl.ds(0, 128), m_ref[...], work)
    lax.fori_loop(0, blocks, block, 0)
    done = last[...]
    m_ref[...] = m_ref[...] - product_tn(done, done)


def window_kernel(part, lead, mine, beside, across, last_piece, *refs):
    high_ref, low_ref, m_ref, diag, v_ref, h_ref, work, ahead, last = refs[-9:]
    first, size = PARTS[part]
    y = lax.rem(lax.axis_index("cand"), 4)
    for b, holders in enumerate(((mine, beside, last_piece, across), (beside, mine, across, last_piece))):
        begin, end = max(first, W * b), min(first + size, W * b + W)
        if begin >= end:
            continue
        for n, holder in enumerate(holders):
            @pl.when(y == n)
            def _():
                v_ref[begin - first:end - first, :] = holder[begin - W * b:end - W * b, :] * 0.0625

    if part:
        m_ref[...] = refs[0][...]
    else:
        square = lambda dim: lax.broadcasted_iota(jnp.int32, (RANK, RANK), dim)
        m_ref[...] = (square(0) == square(1)).astype(F32)
    unpack_tiles(lead[first // 32:(first + size) // 32, :], diag)
    factor_window(diag, v_ref, h_ref, m_ref, work, ahead, last)
    h = h_ref[...]
    high = h.astype(BF16)
    high_ref[...] = high
    low_ref[...] = (h - high.astype(F32)).astype(BF16)


def window_factor(part, lead, v, m):
    vmem = pl.BlockSpec(memory_space=pltpu.VMEM)
    size = PARTS[part][1]
    return pl.pallas_call(
        functools.partial(window_kernel, part),
        in_specs=[vmem] * (5 + len(m)),
        out_specs=[vmem] * 4,
        out_shape=[
            jax.ShapeDtypeStruct((size, RANK), BF16),
            jax.ShapeDtypeStruct((size, RANK), BF16),
            jax.ShapeDtypeStruct((RANK, RANK), F32),
            jax.ShapeDtypeStruct((size, 128), F32),
        ],
        scratch_shapes=[
            pltpu.VMEM((size, RANK), BF16),
            pltpu.VMEM((size, RANK), F32),
            pltpu.VMEM((128, 128 + RANK), F32),
            pltpu.VMEM((128, 128 + RANK), F32),
            pltpu.VMEM((128, RANK), F32),
        ],
        cost_estimate=pl.CostEstimate(flops=size * 10**7, bytes_accessed=size * 10**5, transcendentals=0),
        compiler_params=pltpu.CompilerParams(vmem_limit_bytes=32 * 2**20),
        name="window_factor",
    )(lead, *v, *m)


def rows_kernel(high0, low0, diag0, high1, low1, m_ref, diag1, kept, near, half, own, here, before, after, low, high, out, *scratch):
    own_diag, panel, blocks, sems = scratch
    cand = lax.axis_index("cand")
    x, y = cand // 4, lax.rem(cand, 4)
    v_own = own[...] * 0.0625
    split = PARTS[1][0]
    panel[:, :split] = dot_nt(v_own, high0[...]) + dot_nt(v_own, low0[...])
    panel[:, split:] = dot_nt(v_own, high1[...]) + dot_nt(v_own, low1[...])
    for n in range(2):
        @pl.when(cand == n)
        def _():
            row = lax.broadcasted_iota(jnp.int32, (W, WINDOW), 0) // 128 + 3 * n
            col = lax.broadcasted_iota(jnp.int32, (W, WINDOW), 1) // 128
            panel[...] = jnp.where(row > col, panel[...], 0.0)
            for a in range(3):
                at = W * n + 128 * a
                diag = diag0[at:at + 128, :] if at < split else diag1[at - split:at - split + 128, :]
                panel[128 * a:128 * a + 128, at:at + 128] = diag

    panel_copy = pltpu.make_async_copy(panel, out.at[0, :, pl.ds(0, WINDOW)], sems.at[16])
    panel_copy.start()
    unpack_tiles(kept[...] + near[...] + half[...], own_diag)
    m1, m2, m3 = split3(m_ref[...])
    q = (dot_nn(v_own, m1) + (dot_nn(v_own, m2) + dot_nn(v_own, m3))) * 0.0625
    q = jnp.where(cand < 2, 0.0, q)
    q1 = q.astype(BF16)
    q2 = (q - q1.astype(F32)).astype(BF16)
    q12 = jnp.concatenate([q1, q2], axis=1)
    stores = []
    for n, pieces in enumerate((here, before, after, (low, high))):
        column_y = lax.rem(y + (0, 3, 1, 2)[n], 4)
        for pair in range(2):
            v = pieces[pair][...] if n == 3 else pieces[2 * pair:2 * pair + 2]
            v = v.reshape(2 * W, RANK)
            slot = 2 * n + pair
            blocks[slot] = dot_nt(q12, jnp.concatenate([v, v], axis=1))
            if slot == 0:
                @pl.when(cand >= 2)
                def _():
                    for a in range(3):
                        at = slice(128 * a, 128 * a + 128)
                        blocks[0, at, at] += mirror(own_diag[at, :])

            for m in range(2):
                column = 4 * (x ^ ACROSS[2 * pair + m]) + column_y
                copy = pltpu.make_async_copy(
                    blocks.at[slot, :, pl.ds(W * m, W)],
                    out.at[0, :, pl.ds(pl.multiple_of(column * W, 128), W)],
                    sems.at[2 * slot + m],
                )
                stores.append((column, copy))

                @pl.when(column >= 2)
                def _():
                    copy.start()
    panel_copy.wait()
    for column, copy in stores:
        @pl.when(column >= 2)
        def _():
            copy.wait()


def factor_rows(*operands):
    vmem = pl.BlockSpec(memory_space=pltpu.VMEM)
    return pl.pallas_call(
        rows_kernel,
        in_specs=[vmem] * len(operands),
        out_specs=pl.BlockSpec(memory_space=pltpu.HBM),
        out_shape=jax.ShapeDtypeStruct((1, W, 16 * W), F32),
        scratch_shapes=[
            pltpu.VMEM((W, 128), F32),
            pltpu.VMEM((W, WINDOW), F32),
            pltpu.VMEM((8, W, 2 * W), F32),
            pltpu.SemaphoreType.DMA((17,)),
        ],
        compiler_params=pltpu.CompilerParams(vmem_limit_bytes=40 * 2**20),
        name="factor_rows",
    )(*operands)


def move_y(value, shift):
    return lax.ppermute(value, "cand", [(4 * x + y, 4 * x + (y + shift) % 4) for x in range(4) for y in range(4)])


def swap(value, bits):
    return lax.ppermute(value, "cand", [(i, i ^ bits) for i in range(16)])


def move_back(value, offset):
    return lax.ppermute(value, ("cand", "dom"), [(i, (i - offset) % 128) for i in range(128)])


def local(strain_ops, elem_scale, moduli, elem_block, elem_slot, mass, updates):
    cand = lax.axis_index("cand")
    x, y = cand // 4, cand % 4
    own = updates[0]

    small, row = 0.0, 0
    for part in (elem_scale, moduli, mass):
        rows, width = part.shape
        small = small + lax.pad(part, F32(0), ((row, 8 - row - rows, 0), (0, elem_scale.shape[1] - width, 0)))
        row += rows
    code = elem_block.T * 16 + elem_slot[None, :]
    strain = jnp.transpose(strain_ops, (1, 2, 0, 3))
    steps = strain.shape[3] // CHUNK

    beside = swap(own, 4)
    total = stiffness_tiles(0, steps // 2, strain, small, code, (), (BIN_ROWS,))
    total, beside = lax.optimization_barrier((total, beside))
    here = jnp.stack([own, beside])
    here = jnp.concatenate([here, swap(here, 12)])
    keep, far, two, three = stiffness_tiles(steps // 2, steps // 2, strain, small, code, total, (40, 40, 16, 16))

    far = move_back(far, 1)
    two = move_back(two, 2)
    three = move_back(three, 3)
    far, two, three, here = lax.optimization_barrier((far, two, three, here))
    kept = keep[:12] + far[:12] + two[:12] + three[:12]
    near = keep[12:24] + far[12:24]
    half = keep[24:36] + far[24:36]
    zero = jnp.zeros_like(kept)
    pick = lambda c: jnp.where(cand == c, kept, jnp.where(cand == c + 1, near, jnp.where(cand == c + 8, half, zero)))
    lead = jnp.concatenate([pick(0), pick(1)], axis=0)
    mine = functools.reduce(lambda u, n: jnp.where(x == ACROSS[n], here[n], u), range(1, 4), here[0])
    paired, crossed = swap(mine, 1), swap(mine, 3)
    lead = lead + swap(lead, 4)
    lead = lead + swap(lead, 12)
    lead, paired, crossed, near, half = lax.optimization_barrier((lead, paired, crossed, near, half))
    near, half = move_back(near, 8), move_back(half, 64)
    last_piece = swap(crossed, 1)
    lead = lead + swap(lead, 3)
    lead = lead + swap(lead, 1)
    lead, last_piece, here = lax.optimization_barrier((lead, last_piece, here))

    before, after = move_y(here, 1), move_y(here, 3)
    window = (mine, paired, crossed, last_piece)
    high0, low0, m, diag0 = window_factor(0, lead, window, ())
    m, before, after, near, half = lax.optimization_barrier((m, before, after, near, half))
    low, high = move_y(before[:2], 1), move_y(after[2:], 3)
    high1, low1, m, diag1 = window_factor(1, lead, window, (m,))
    return factor_rows(high0, low0, diag0, high1, low1, m, diag1, kept, near, half, own, here, before, after, low, high)


def solution(mesh):
    placed = (
        P(None, None, None, ("cand", "dom")),
        P(None, ("cand", "dom")),
        P(None, ("cand", "dom")),
        P(("cand", "dom"), None),
        P(("cand", "dom")),
        P("dom", "cand"),
        P("dom", "cand", None),
    )
    return jax.shard_map(
        local, mesh=mesh, in_specs=placed, out_specs=P("dom", "cand", None), check_vma=False
    )
```
